32 devices in a mesh: dp: 2 (over core), ctx: 4 (over z), mp: 4 (over y, x).
Axes of the slice: x: 2, y: 2, z: 4, core: 2. Of those that a mesh axis runs over, the one named last changes fastest.
Arguments:
- tokens: bfloat16 [2, 2048, 1024], P('dp', ('ctx', 'mp')), may hold values from -6 to 6
- norm1_gain: bfloat16 [1024], replicated, may hold values from 0.5 to 1.5
- q_weight: bfloat16 [1024, 2048], P(None, 'mp'), may hold values from -0.1875 to 0.1875
- key_matrix: bfloat16 [1024, 1024], P(None, 'mp'), may hold values from -0.1875 to 0.1875
- value_matrix: bfloat16 [1024, 1024], P(None, 'mp'), may hold values from -0.1875 to 0.1875
- q_gain: bfloat16 [128], replicated, may hold values from 0.5 to 1.5
- k_gain: bfloat16 [128], replicated, may hold values from 0.5 to 1.5
- o_weight: bfloat16 [2048, 1024], P('mp'), may hold values from -2 to 2
- norm2_gain: bfloat16 [1024], replicated, may hold values from 0.5 to 1.5
- gate_weight: bfloat16 [1024, 3072], P(None, 'mp'), may hold values from -0.1875 to 0.1875
- up_weight: bfloat16 [1024, 3072], P(None, 'mp'), may hold values from -0.1875 to 0.1875
- down_weight: bfloat16 [3072, 1024], P('mp'), may hold values from -0.109375 to 0.109375
- out_grad: bfloat16 [2, 2048, 1024], P('dp', ('ctx', 'mp')), may hold values from -6 to 6
- lengths: int32 [2, 4], P('dp'), may hold values from 1 to 2045, as said below
- pairing: int32 [4], replicated, may hold values from 0 to 3, each once
Outputs:
- output: bfloat16 [2, 2048, 1024], P('dp', ('ctx', 'mp'))
- input_grad: float32 [2, 2048, 1024], P('dp', ('ctx', 'mp'))
- norm1_gain_grad: float32 [1024], replicated
- q_weight_grad: float32 [1024, 2048], P(None, 'mp')
- k_weight_grad: float32 [1024, 1024], P(None, 'mp')
- v_weight_grad: float32 [1024, 1024], P(None, 'mp')
- q_gain_grad: float32 [128], replicated
- k_gain_grad: float32 [128], replicated
- o_weight_grad: float32 [2048, 1024], P('mp')
- norm2_gain_grad: float32 [1024], replicated
- gate_weight_grad: float32 [1024, 3072], P(None, 'mp')
- up_weight_grad: float32 [1024, 3072], P(None, 'mp')
- down_weight_grad: float32 [3072, 1024], P('mp')
The draws below stay inside these ranges and needn't reach their ends.
Inputs may be any that keep to these rules, and one draw needn't show every extreme that they name: `lengths`: each row sums to 2048; one document of each row, at a place drawn from the seed, holds all but at most 128 of its tokens; in one row, drawn from the seed, every other document holds one token. Ctx device c holds blocks pairing[c] and 7 - pairing[c] of its sequence.
All inputs are finite; a program needn't handle non-finite values.
Results may differ from the reference program's by a relative error of at most 0.024.
Values may be sent and summed in bfloat16 or wider, within the bound.
No kernel may reach another device: no remote copies, remote signals or barrier semaphores. Data moves between devices by JAX's collectives and lax.ppermute only.
A program may use at most 256 MiB of HBM per device.

```python
import math
import jax
import jax.numpy as jnp
from jax import lax

MODEL_DIM = 1024
QUERY_HEADS = 16
KEY_VALUE_HEADS = 8
HEAD_SIZE = 128
FF = 3072
BLK = 256
DOCS = 4
SEQUENCE_TOKENS = 2048
SEQS = 2
N_CTX = 4


def draw_lengths(key, part):
    key = jax.random.fold_in(key, 11)
    short_key, place_key, row_key = jax.random.split(key, 3)
    short_most = max(1, BLK // (2 * (DOCS - 1)))
    shorts = jax.random.randint(short_key, (SEQS, DOCS - 1), 1, short_most + 1)
    single_row = jax.random.randint(row_key, (), 0, SEQS)
    row_ids = jnp.arange(SEQS, dtype=jnp.int32)[:, None]
    shorts = jnp.where(row_ids == single_row, 1, shorts)
    longest = SEQUENCE_TOKENS - jnp.sum(shorts, axis=1, keepdims=True)
    long_place = jax.random.randint(place_key, (SEQS, 1), 0, DOCS)
    columns = jnp.arange(DOCS, dtype=jnp.int32)[None, :]
    source = jnp.clip(columns - (columns > long_place).astype(jnp.int32), 0, DOCS - 2)
    picked = jnp.take_along_axis(shorts, jnp.broadcast_to(source, (SEQS, DOCS)), axis=1)
    return jnp.where(columns == long_place, longest, picked).astype(jnp.int32)


def shard_levels(rng, dims, shards, least, top_value):
    loudness, own = 1.0, jax.random.fold_in(rng, 6)
    for position, shards_of in shards:
        heights = jnp.exp(jax.random.uniform(jax.random.fold_in(own, position), (shards_of,), jnp.float32, least / len(shards), top_value / len(shards)))
        loudness = loudness * jnp.repeat(heights, dims[position] // shards_of).reshape([-1 if axis == position else 1 for axis in range(len(dims))])
    return loudness


def bell_draw(stream_key, extent, spread, reach, shards=(), kind=jnp.bfloat16):
    drawn = spread * jax.random.normal(stream_key, extent, jnp.float32)
    if shards:
        drawn = drawn * shard_levels(stream_key, extent, shards, -0.22, 0.18)
    return jnp.clip(drawn, -reach, reach).astype(kind)


def setup_inputs(seed: int = 0) -> dict:
    keys = jax.random.split(jax.random.key(seed), 16)
    tokens = bell_draw(keys[0], (SEQS, SEQUENCE_TOKENS, MODEL_DIM), 1.0, 6.0, ((0, 2), (1, 16)))
    norm1_gain = jnp.clip(1.0 + 0.1 * jax.random.normal(keys[1], (MODEL_DIM,), jnp.float32), 0.5, 1.5).astype(jnp.bfloat16)
    q_weight = bell_draw(keys[2], (MODEL_DIM, QUERY_HEADS * HEAD_SIZE), MODEL_DIM ** -0.5, 0.1875, ((1, 4),))
    key_matrix = bell_draw(keys[3], (MODEL_DIM, KEY_VALUE_HEADS * HEAD_SIZE), MODEL_DIM ** -0.5, 0.1875, ((1, 4),))
    value_matrix = bell_draw(keys[4], (MODEL_DIM, KEY_VALUE_HEADS * HEAD_SIZE), MODEL_DIM ** -0.5, 0.1875, ((1, 4),))
    q_gain = jnp.clip(1.0 + 0.1 * jax.random.normal(keys[5], (HEAD_SIZE,), jnp.float32), 0.5, 1.5).astype(jnp.bfloat16)
    k_gain = jnp.clip(1.0 + 0.1 * jax.random.normal(keys[6], (HEAD_SIZE,), jnp.float32), 0.5, 1.5).astype(jnp.bfloat16)
    o_weight = bell_draw(keys[7], (QUERY_HEADS * HEAD_SIZE, MODEL_DIM), (max(1, QUERY_HEADS * HEAD_SIZE * 8 // SEQUENCE_TOKENS)) ** -0.5, 2.0, ((0, 4),))
    norm2_gain = jnp.clip(1.0 + 0.1 * jax.random.normal(keys[8], (MODEL_DIM,), jnp.float32), 0.5, 1.5).astype(jnp.bfloat16)
    gate_weight = bell_draw(keys[9], (MODEL_DIM, FF), MODEL_DIM ** -0.5, 0.1875, ((1, 4),))
    up_weight = bell_draw(keys[10], (MODEL_DIM, FF), MODEL_DIM ** -0.5, 0.1875, ((1, 4),))
    down_weight = bell_draw(keys[11], (FF, MODEL_DIM), FF ** -0.5, 0.109375, ((0, 4),))
    out_grad = bell_draw(keys[12], (SEQS, SEQUENCE_TOKENS, MODEL_DIM), 1.0, 6.0, ((0, 2), (1, 16)))
    lengths = draw_lengths(jax.random.fold_in(keys[15], 71), 0)
    pairing = jax.random.permutation(keys[14], N_CTX).astype(jnp.int32)
    return {"tokens": tokens, "norm1_gain": norm1_gain, "q_weight": q_weight, "key_matrix": key_matrix, "value_matrix": value_matrix, "q_gain": q_gain, "k_gain": k_gain, "o_weight": o_weight, "norm2_gain": norm2_gain, "gate_weight": gate_weight, "up_weight": up_weight, "down_weight": down_weight, "out_grad": out_grad, "lengths": lengths, "pairing": pairing}


@jax.custom_vjp
def reduced_precision(v):
    return lax.optimization_barrier(v.astype(jnp.bfloat16)).astype(jnp.float32)

@jax.custom_vjp
def reduced_precision_back(v):
    return v

def low_keep(v):
    return (reduced_precision(v), None)

def low_pass(kept, grad):
    return (grad,)

def back_keep(v):
    return (v, None)

def back_low(kept, grad):
    return (reduced_precision(grad),)
reduced_precision.defvjp(low_keep, low_pass)
reduced_precision_back.defvjp(back_keep, back_low)
HIGH = lax.Precision.HIGHEST
EPS = 1e-06
THETA = 1000000.0
NEG = -1e+30

def matrix_product(left, right):
    return jnp.dot(left, right, precision=HIGH)

def norm_rows(value_rows, gain):
    return value_rows * lax.rsqrt(lax.optimization_barrier(jnp.mean(value_rows * value_rows, axis=-1, keepdims=True)) + EPS) * gain

def turn_half(value_rows):
    half_width = value_rows.shape[-1] // 2
    return jnp.concatenate([-value_rows[..., half_width:], value_rows[..., :half_width]], axis=-1)

def rope_tables(token_positions):
    half_width = HEAD_SIZE // 2
    frequency = THETA ** (-(jnp.arange(half_width, dtype=jnp.float32) * 2.0) / HEAD_SIZE)
    angles = token_positions.astype(jnp.float32)[:, None] * frequency[None, :]
    cosines = jnp.concatenate([jnp.cos(angles), jnp.cos(angles)], axis=-1)
    sines = jnp.concatenate([jnp.sin(angles), jnp.sin(angles)], axis=-1)
    return (cosines, sines)

def rotate(value_rows, cosines, sines):
    return value_rows * cosines[:, None, :] + turn_half(value_rows) * sines[:, None, :]

def layout_positions(pairing):
    rows_all = jnp.arange(SEQUENCE_TOKENS, dtype=jnp.int32)
    owners = rows_all // (2 * BLK)
    paired = pairing[owners]
    chosen = jnp.where(rows_all % (2 * BLK) < BLK, paired, 2 * N_CTX - 1 - paired)
    return (chosen * BLK + rows_all % BLK).astype(jnp.int32)

def doc_numbers(doc_lengths, token_positions):
    doc_ends = jnp.cumsum(doc_lengths)
    return lax.optimization_barrier(jnp.sum((token_positions[:, None] >= doc_ends[None, :]).astype(jnp.int32), axis=1))

def attend_rows(query_rows, key_rows, value_rows, token_positions, document_list):
    group_width = QUERY_HEADS // KEY_VALUE_HEADS
    query_tile_block = min(512, SEQUENCE_TOKENS)
    token_count = SEQUENCE_TOKENS // query_tile_block
    score_scale = 1.0 / math.sqrt(HEAD_SIZE)
    query_blocks = query_rows.reshape(token_count, query_tile_block, KEY_VALUE_HEADS, group_width, HEAD_SIZE)
    pos_blocks = token_positions.reshape(token_count, query_tile_block)
    doc_blocks = document_list.reshape(token_count, query_tile_block)

    def one_block(pieces):
        q_piece, pos_piece, doc_piece = pieces
        raw_scores = reduced_precision_back(jnp.einsum('qhgd,khd->hgqk', q_piece, key_rows, precision=HIGH) * score_scale)
        allowed = (token_positions[None, :] <= pos_piece[:, None]) & (document_list[None, :] == doc_piece[:, None])
        masked = jnp.where(allowed, raw_scores, NEG)
        row_top = lax.optimization_barrier(jnp.max(masked, axis=-1, keepdims=True))
        exponent = jnp.exp(masked - row_top)
        row_total = lax.optimization_barrier(jnp.sum(exponent, axis=-1))
        numer = reduced_precision_back(jnp.einsum('hgqk,khd->qhgd', reduced_precision(exponent), value_rows, precision=HIGH))
        return numer / jnp.transpose(row_total, (2, 0, 1))[..., None]
    out_blocks = lax.map(jax.checkpoint(one_block), (query_blocks, pos_blocks, doc_blocks))
    return out_blocks.reshape(SEQUENCE_TOKENS, QUERY_HEADS * HEAD_SIZE)

def layer_forward(rows, weights, token_positions, document_list):
    norm1_gain, q_weight, key_matrix, value_matrix, q_gain, k_gain, o_weight, norm2_gain, gate_weight, up_weight, down_weight = weights
    hidden_first = reduced_precision(norm_rows(rows, norm1_gain))
    q_lin = reduced_precision_back(matrix_product(hidden_first, q_weight)).reshape(SEQUENCE_TOKENS, QUERY_HEADS, HEAD_SIZE)
    key_linear = reduced_precision_back(matrix_product(hidden_first, key_matrix)).reshape(SEQUENCE_TOKENS, KEY_VALUE_HEADS, HEAD_SIZE)
    value_rows = reduced_precision(reduced_precision_back(matrix_product(hidden_first, value_matrix))).reshape(SEQUENCE_TOKENS, KEY_VALUE_HEADS, HEAD_SIZE)
    cosines, sines = rope_tables(token_positions)
    query_rows = reduced_precision(rotate(norm_rows(q_lin, q_gain), cosines, sines))
    key_rows = reduced_precision(rotate(norm_rows(key_linear, k_gain), cosines, sines))
    attended_output = attend_rows(query_rows.reshape(SEQUENCE_TOKENS, KEY_VALUE_HEADS, QUERY_HEADS // KEY_VALUE_HEADS, HEAD_SIZE), key_rows, value_rows, token_positions, document_list)
    attended_output = reduced_precision_back(reduced_precision(attended_output))
    resid = rows + reduced_precision_back(matrix_product(attended_output, o_weight))
    hidden2 = reduced_precision(norm_rows(resid, norm2_gain))
    gate = reduced_precision_back(matrix_product(hidden2, gate_weight))
    up_val = reduced_precision_back(matrix_product(hidden2, up_weight))
    activ = reduced_precision(jax.nn.silu(gate) * up_val)
    return resid + matrix_product(activ, down_weight)

def reference(tokens, norm1_gain, q_weight, key_matrix, value_matrix, q_gain, k_gain, o_weight, norm2_gain, gate_weight, up_weight, down_weight, out_grad, lengths, pairing):
    token_positions = layout_positions(pairing)
    weights = tuple((item.astype(jnp.float32) for item in (norm1_gain, q_weight, key_matrix, value_matrix, q_gain, k_gain, o_weight, norm2_gain, gate_weight, up_weight, down_weight)))
    tokens_f = tokens.astype(jnp.float32)

    def forward(rows_all, weight_set):

        def one_sequence(pieces):
            rows, doc_lengths = pieces
            document_list = doc_numbers(doc_lengths, token_positions)
            return layer_forward(rows, weight_set, token_positions, document_list)
        return lax.map(one_sequence, (rows_all, lengths))
    output, pullback = jax.vjp(forward, tokens_f, weights)
    input_grad, weight_grads = pullback(out_grad.astype(jnp.float32))
    return (output.astype(jnp.bfloat16), input_grad, weight_grads[0], weight_grads[1], weight_grads[2], weight_grads[3], weight_grads[4], weight_grads[5], weight_grads[6], weight_grads[7], weight_grads[8], weight_grads[9], weight_grads[10])
```

```python
import math

import jax
import jax.numpy as jnp
from jax import lax
from jax.experimental import pallas as pl
from jax.experimental.pallas import tpu as pltpu
from jax.sharding import PartitionSpec as P

EPS = 1e-06
THETA = 1000000.0
LOG2E = 1.4426950408889634
BF = jnp.bfloat16
F32 = jnp.float32
VMEM_LIMIT = 52 * 1024 * 1024


def dot(left, right, left_dim, right_dim):
    return lax.dot_general(
        left, right, (((left_dim,), (right_dim,)), ((), ())), preferred_element_type=F32
    )


def whole_spec(array):
    rank = len(array.shape)
    return pl.BlockSpec(array.shape, lambda *_: (0,) * rank)


SMEM = pl.BlockSpec(memory_space=pltpu.SMEM)


def call(kernel, ins, outs, grid=(1,), in_specs=None, out_specs=None, scratch=(), flops=0, name=None):
    in_specs = in_specs or {}
    out_specs = out_specs or {}
    moved = sum(math.prod(a.shape) * a.dtype.itemsize for a in list(ins) + list(outs))
    return pl.pallas_call(
        kernel,
        grid=grid,
        in_specs=[in_specs.get(i, whole_spec(a)) for i, a in enumerate(ins)],
        out_specs=[out_specs.get(i, whole_spec(a)) for i, a in enumerate(outs)],
        out_shape=list(outs),
        scratch_shapes=list(scratch),
        compiler_params=pltpu.CompilerParams(vmem_limit_bytes=VMEM_LIMIT),
        cost_estimate=pl.CostEstimate(flops=flops, bytes_accessed=moved, transcendentals=0),
        name=name,
    )(*ins)


def out(shape, dtype):
    return jax.ShapeDtypeStruct(shape, dtype)


def swap(value, axis, step):
    size = lax.axis_size(axis)
    return lax.ppermute(value, axis, [(i, i ^ step) for i in range(size)])


def swaps(values, axis):
    order = sorted(range(1, len(values)), key=lambda j: -bin(j).count("1"))
    got = {j: swap(values[j], axis, j) for j in order}
    return [got[j] for j in range(1, len(values))]


def from_ctx(value, step):
    size = lax.axis_size("ctx")
    return lax.ppermute(value, "ctx", [((i + step) % size, i) for i in range(size)])


def to_ctx(value, step):
    size = lax.axis_size("ctx")
    return lax.ppermute(value, "ctx", [(i, (i + step) % size) for i in range(size)])


def norm_kernel(rows_ref, gain_ref, normed_ref):
    rows = rows_ref[...].astype(F32)
    factor = lax.rsqrt(jnp.mean(rows * rows, axis=-1, keepdims=True) + EPS)
    normed_ref[...] = (rows * factor * gain_ref[...]).astype(BF)


def resid_kernel(tok_ref, own_ref, *refs):
    *parts, gain_ref, resid_ref, normed_ref = refs
    rows = tok_ref[...].astype(F32) + own_ref[...]
    for part in parts:
        rows = rows + part[...].astype(F32)
    resid_ref[...] = rows
    factor = lax.rsqrt(jnp.mean(rows * rows, axis=-1, keepdims=True) + EPS)
    normed_ref[...] = (rows * factor * gain_ref[...]).astype(BF)


def norm_back(rows, gain, gradient):
    factor = lax.rsqrt(jnp.mean(rows * rows, axis=-1, keepdims=True) + EPS)
    scaled = gradient * gain
    inner = jnp.mean(scaled * rows, axis=-1, keepdims=True)
    return factor * scaled - rows * (factor * factor * factor) * inner, gradient * rows * factor


def resid_back_kernel(resid_ref, grad_ref, gain_ref, own_ref, *refs):
    *parts, full_ref, low_ref, gain_grad_ref = refs
    gradient = own_ref[...]
    for part in parts:
        gradient = gradient + part[...].astype(F32)
    back, terms = norm_back(resid_ref[...], gain_ref[...], gradient)
    total = grad_ref[...].astype(F32) + back
    full_ref[...] = total
    low_ref[...] = total.astype(BF)
    gain_grad_ref[...] = jnp.sum(terms, axis=0, keepdims=True)


def input_back_kernel(tok_ref, resid_grad_ref, gain_ref, *refs):
    *parts, result_ref = refs
    gradient = parts[0][...].astype(F32)
    for part in parts[1:]:
        gradient = gradient + part[...].astype(F32)
    back, _ = norm_back(tok_ref[...].astype(F32), gain_ref[...], gradient)
    result_ref[...] = resid_grad_ref[...] + back


def sum_kernel(*refs):
    *parts, result_ref = refs
    total = parts[0][...].astype(F32)
    for part in parts[1:]:
        total = total + part[...].astype(F32)
    result_ref[...] = total.astype(result_ref.dtype)


def sum_parts(parts, dtype):
    return call(sum_kernel, parts, [out(parts[0].shape, dtype)], name="sum_parts")[0]


def key_rows(linear, gain, cosines, sines):
    heads = []
    for start in range(0, linear.shape[1], gain.shape[1]):
        rows = linear[:, start : start + gain.shape[1]]
        factor = lax.rsqrt(jnp.mean(rows * rows, axis=-1, keepdims=True) + EPS)
        normed = rows * factor * gain
        turned = pltpu.roll(normed, normed.shape[1] // 2, 1)
        heads.append((normed * cosines + turned * sines).astype(BF))
    return heads


def key_value_part(hidden, wk_ref, wv_ref, gk_ref, cos_ref, sin_ref, k_ref, v_ref, klin_ref):
    linear = dot(hidden, wk_ref[...], 1, 0)
    klin_ref[...] = linear
    width = gk_ref.shape[1]
    for head, rows in enumerate(key_rows(linear, gk_ref[...], cos_ref[...], sin_ref[...])):
        k_ref[:, head * width : (head + 1) * width] = rows
    v_ref[...] = dot(hidden, wv_ref[...], 1, 0).astype(BF)


def turn_rows(value):
    half = value.shape[0] // 2
    return jnp.concatenate([-value[half:], value[:half]], axis=0)


def own_kernel(count, *refs):
    parts = refs[:count]
    (wq_ref, wk_ref, wv_ref, gq_ref, gk_ref, cos_t_ref, sin_t_ref, cos_ref, sin_ref) = refs[
        count : count + 9
    ]
    qt_ref, qlin_ref, k_ref, v_ref, klin_ref, hidden_ref = refs[count + 9 :]
    share = parts[0].shape[0]
    for j, part in enumerate(parts):
        hidden_ref[j * share : (j + 1) * share, :] = part[...]
    hidden = hidden_ref[...]
    key_value_part(hidden, wk_ref, wv_ref, gk_ref, cos_ref, sin_ref, k_ref, v_ref, klin_ref)
    linear = dot(wq_ref[...], hidden, 0, 1)
    qlin_ref[...] = linear
    width = gq_ref.shape[0]
    for start in range(0, linear.shape[0], width):
        rows = linear[start : start + width]
        factor = lax.rsqrt(jnp.mean(rows * rows, axis=0, keepdims=True) + EPS)
        normed = rows * factor * gq_ref[...]
        qt_ref[start : start + width, :] = (
            normed * cos_t_ref[...] + turn_rows(normed) * sin_t_ref[...]
        ).astype(BF)


def remote_kernel(count, *refs):
    parts = refs[:count]
    wk_ref, wv_ref, gk_ref, cos_ref, sin_ref = refs[count : count + 5]
    k_ref, v_ref, klin_ref, hidden_ref = refs[count + 5 :]
    share = parts[0].shape[1]
    for j, part in enumerate(parts):
        hidden_ref[j * share : (j + 1) * share, :] = part[0]
    key_value_part(
        hidden_ref[...], wk_ref, wv_ref, gk_ref, cos_ref, sin_ref, k_ref, v_ref, klin_ref
    )


def place_slots(target_ref, refs, groups, rows):
    if len(refs) == 1:
        return refs[0]
    for ref, group in zip(refs, groups):
        for i, slot in enumerate(group):
            target_ref[pl.ds(slot * rows, rows), :] = ref[i * rows : (i + 1) * rows, :]
    return target_ref


def lanes_of(ref, half_index, half, width):
    heads = [
        ref[start : start + width, half_index * half : (half_index + 1) * half]
        for start in range(0, ref.shape[0], width)
    ]
    return jnp.concatenate(heads, axis=1)


def attend_kernel(groups, ctx_rows, width, mp, *refs):
    n = len(groups)
    order_ref, last_ref, kpos_ref, qpos_ref, qlow_ref, qt_ref, wo_ref = refs[:7]
    k_refs, v_refs = refs[7 : 7 + n], refs[7 + n : 7 + 2 * n]
    rest = refs[7 + 2 * n :]
    ot_ref, attt_ref, sums_ref = rest[:3]
    part_refs = rest[3 : 3 + mp]
    k_all, v_all, numer, sums, projected = rest[3 + mp :]
    half = ctx_rows // 2
    share = ctx_rows // mp
    per_group = qt_ref.shape[0] // width
    k_all = place_slots(k_all, k_refs, groups, ctx_rows)
    v_all = place_slots(v_all, v_refs, groups, ctx_rows)
    scale = LOG2E / math.sqrt(width)
    for t in range(2):
        queries = lanes_of(qt_ref, t, half, width)
        qpos = jnp.concatenate([qpos_ref[:, t * half : (t + 1) * half]] * per_group, axis=1)
        qlow = jnp.concatenate([qlow_ref[:, t * half : (t + 1) * half]] * per_group, axis=1)
        numer[...] = jnp.zeros_like(numer)
        sums[...] = jnp.zeros_like(sums)

        def step(i, carry):
            start = pl.multiple_of(order_ref[i] * half, half)
            scores = dot(k_all[pl.ds(start, half), :], queries, 1, 0)
            kpos = kpos_ref[...] + i * half
            seen = (kpos <= qpos) & (kpos >= qlow)
            weights = jnp.where(seen, jnp.exp2(scores * scale), 0.0)
            sums[...] += jnp.sum(weights, axis=0, keepdims=True)
            numer[...] += dot(v_all[pl.ds(start, half), :], weights.astype(BF), 0, 0)
            return carry

        lax.fori_loop(0, last_ref[t] + 1, step, 0)
        total = sums[...]
        sums_ref[0, t : t + 1, :] = total
        result = numer[...] / total
        for head in range(per_group):
            piece = result[:, head * half : (head + 1) * half]
            ot_ref[head * width : (head + 1) * width, t * half : (t + 1) * half] = piece
            attt_ref[head * width : (head + 1) * width, t * half : (t + 1) * half] = piece.astype(BF)
    added = dot(attt_ref[...], wo_ref[...], 0, 0)
    group = pl.program_id(0)

    @pl.when(group == 0)
    def _():
        projected[...] = added

    @pl.when(group > 0)
    def _():
        projected[...] += added

    @pl.when(group == pl.num_programs(0) - 1)
    def _():
        for j, ref in enumerate(part_refs):
            ref[...] = projected[j * share : (j + 1) * share, :].astype(ref.dtype)


def feed_kernel(count, *refs):
    peer_ref = refs[0]
    parts = refs[1 : 1 + count]
    grad_ref, wg_ref, wu_ref, wd_ref = refs[1 + count : 5 + count]
    hidden_ref, grads_ref, act_ref, gg_ref, ug_ref = refs[5 + count : 10 + count]
    part_refs = refs[10 + count : 10 + 2 * count]
    total = refs[10 + 2 * count]
    share = parts[0].shape[0]
    step = pl.program_id(0)

    @pl.when(step == 0)
    def _():
        for j, part in enumerate(parts):
            hidden_ref[j * share : (j + 1) * share, :] = part[...]
            place = pl.multiple_of(peer_ref[j] * share, share)
            grads_ref[j * share : (j + 1) * share, :] = grad_ref[pl.ds(place, share), :]

    hidden = hidden_ref[...]
    gate = dot(hidden, wg_ref[...], 1, 0)
    up = dot(hidden, wu_ref[...], 1, 0)
    act_grad = dot(grads_ref[...], wd_ref[...], 1, 1)
    sig = 1.0 / (1.0 + jnp.exp(-gate))
    silu = gate * sig
    act_ref[...] = (silu * up).astype(BF)
    gate_grad = (act_grad * up * sig * (1.0 + gate * (1.0 - sig))).astype(BF)
    up_grad = (act_grad * silu).astype(BF)
    gg_ref[...] = gate_grad
    ug_ref[...] = up_grad
    added = dot(gate_grad, wg_ref[...], 1, 1) + dot(up_grad, wu_ref[...], 1, 1)

    @pl.when(step == 0)
    def _():
        total[...] = added

    @pl.when(step > 0)
    def _():
        total[...] += added

    @pl.when(step == pl.num_programs(0) - 1)
    def _():
        for j, ref in enumerate(part_refs):
            ref[...] = total[j * share : (j + 1) * share, :].astype(ref.dtype)


def feed_weights_kernel(hidden_ref, grads_ref, act_ref, gg_ref, ug_ref, wd_ref, *refs):
    dg_ref, du_ref, dd_ref = refs[:3]
    *part_refs, total = refs[3:]
    share = part_refs[0].shape[0]
    step = pl.program_id(0)
    dg_ref[...] = dot(hidden_ref[...], gg_ref[...], 0, 0).astype(BF)
    du_ref[...] = dot(hidden_ref[...], ug_ref[...], 0, 0).astype(BF)
    dd_ref[...] = dot(act_ref[...], grads_ref[...], 0, 0).astype(BF)
    added = dot(act_ref[...], wd_ref[...], 1, 0)

    @pl.when(step == 0)
    def _():
        total[...] = added

    @pl.when(step > 0)
    def _():
        total[...] += added

    @pl.when(step == pl.num_programs(0) - 1)
    def _():
        for j, ref in enumerate(part_refs):
            ref[...] = total[j * share : (j + 1) * share, :].astype(ref.dtype)


def attend_back_kernel(groups, ctx_rows, width, mp, *refs):
    n = len(groups)
    order_ref, last_ref, kpos_ref, qpos_ref, qlow_ref = refs[:5]
    low_refs = refs[5 : 5 + mp]
    wo_ref, qt_ref, qlin_ref, ot_ref, sums_ref, gq_ref, cos_t_ref, sin_t_ref = refs[
        5 + mp : 13 + mp
    ]
    at = 13 + mp
    k_refs, v_refs = refs[at : at + n], refs[at + n : at + 2 * n]
    at += 2 * n
    ql_ref, dk, dv, gqg_ref = refs[at : at + 4]
    k_all, v_all, dq, low_all, dqt = refs[at + 4 :]
    half = ctx_rows // 2
    share = ctx_rows // mp
    per_group = qt_ref.shape[0] // width
    scale = LOG2E / math.sqrt(width)
    score_scale = 1.0 / math.sqrt(width)
    group = pl.program_id(0)
    k_all = place_slots(k_all, k_refs, groups, ctx_rows)
    v_all = place_slots(v_all, v_refs, groups, ctx_rows)
    dk[...] = jnp.zeros_like(dk)
    dv[...] = jnp.zeros_like(dv)

    @pl.when(group == 0)
    def _():
        for j, ref in enumerate(low_refs):
            low_all[j * share : (j + 1) * share, :] = ref[...]
        gqg_ref[...] = jnp.zeros_like(gqg_ref)

    att_grad = dot(wo_ref[...], low_all[...], 1, 1).astype(BF).astype(F32)
    for t in range(2):
        queries = lanes_of(qt_ref, t, half, width)
        pre = lanes_of(ot_ref, t, half, width)
        grads = jnp.concatenate(
            [
                att_grad[h * width : (h + 1) * width, t * half : (t + 1) * half]
                for h in range(per_group)
            ],
            axis=1,
        )
        inverse = 1.0 / sums_ref[0, t : t + 1, :]
        scaled = (grads * inverse).astype(BF)
        shift = jnp.sum(grads * pre, axis=0, keepdims=True) * inverse
        qpos = jnp.concatenate([qpos_ref[:, t * half : (t + 1) * half]] * per_group, axis=1)
        qlow = jnp.concatenate([qlow_ref[:, t * half : (t + 1) * half]] * per_group, axis=1)
        dq[...] = jnp.zeros_like(dq)

        def step(i, carry):
            start = pl.multiple_of(order_ref[i] * half, half)
            keys = k_all[pl.ds(start, half), :]
            scores = dot(keys, queries, 1, 0)
            prob_grad = dot(v_all[pl.ds(start, half), :], scaled, 1, 0)
            kpos = kpos_ref[...] + i * half
            seen = (kpos <= qpos) & (kpos >= qlow)
            weights = jnp.where(seen, jnp.exp2(scores * scale), 0.0)
            score_grad = (weights * (prob_grad - shift)).astype(BF)
            dv[pl.ds(start, half), :] += dot(weights.astype(BF), scaled, 1, 1)
            dk[pl.ds(start, half), :] += dot(score_grad, queries, 1, 1)
            dq[...] += dot(keys, score_grad, 0, 0)
            return carry

        lax.fori_loop(0, last_ref[t] + 1, step, 0)
        for head in range(per_group):
            dqt[head * width : (head + 1) * width, t * half : (t + 1) * half] = dq[
                :, head * half : (head + 1) * half
            ]
    for head in range(per_group):
        rows = qlin_ref[head * width : (head + 1) * width, :]
        rotated = dqt[head * width : (head + 1) * width, :] * score_scale
        gradient = rotated * cos_t_ref[...] - turn_rows(rotated) * sin_t_ref[...]
        factor = lax.rsqrt(jnp.mean(rows * rows, axis=0, keepdims=True) + EPS)
        gained = gradient * gq_ref[...]
        inner = jnp.mean(gained * rows, axis=0, keepdims=True)
        ql_ref[head * width : (head + 1) * width, :] = (
            factor * gained - rows * (factor * factor * factor) * inner
        ).astype(BF)
        gqg_ref[...] += jnp.sum(gradient * rows * factor, axis=1, keepdims=True)


def hidden_back_kernel(own, mp, *refs):
    if own:
        ql_ref, wq_ref, *refs = refs
    dk_ref, dv_ref, klin_ref, cos_ref, sin_ref, gk_ref, wk_ref, wv_ref = refs[:8]
    kl_ref, vl_ref, gkg_ref = refs[8:11]
    part_refs = refs[11:]
    share = part_refs[0].shape[1]
    width = gk_ref.shape[1]
    score_scale = 1.0 / math.sqrt(width)

    @pl.when(pl.program_id(0) == 0)
    def _():
        gkg_ref[...] = jnp.zeros_like(gkg_ref)

    for start in range(0, dk_ref.shape[1], width):
        head = slice(start, start + width)
        rotated = dk_ref[:, head] * score_scale
        gradient = rotated * cos_ref[...] - pltpu.roll(rotated, width // 2, 1) * sin_ref[...]
        back, terms = norm_back(klin_ref[:, head], gk_ref[...], gradient)
        kl_ref[:, head] = back.astype(BF)
        gkg_ref[...] += jnp.sum(terms, axis=0, keepdims=True)
    vl_ref[...] = dv_ref[...].astype(BF)
    total = dot(kl_ref[...], wk_ref[...], 1, 1) + dot(vl_ref[...], wv_ref[...], 1, 1)
    if own:
        total = total + dot(ql_ref[...], wq_ref[...], 0, 1)
    for j, ref in enumerate(part_refs):
        ref[0] = total[j * share : (j + 1) * share, :].astype(ref.dtype)


def weights_kernel(groups, mp, *refs):
    n = len(groups)
    core_ref, ql_ref, attt_ref = refs[:3]
    hidden_refs, kl_refs, vl_refs = refs[3 : 3 + n], refs[3 + n : 3 + 2 * n], refs[3 + 2 * n : 3 + 3 * n]
    low_refs = refs[3 + 3 * n : 3 + 3 * n + mp]
    wq_ref, wk_ref, wv_ref, gain_ref, mine_ref, other_ref, gain_grad_ref, accum, low_all, keep = refs[
        3 + 3 * n + mp :
    ]
    step = pl.program_id(0)
    model = gain_ref.shape[0]
    q_width, k_width = ql_ref.shape[0], kl_refs[0].shape[1]
    share = low_refs[0].shape[0]

    @pl.when(step == 0)
    def _():
        for j, ref in enumerate(low_refs):
            low_all[j * share : (j + 1) * share, :] = ref[...]
        keep[:model, :q_width] = dot(hidden_refs[0][...], ql_ref[...], 0, 1)
        keep[model:, :] = dot(attt_ref[...], low_all[...], 1, 0)
        accum[...] = jnp.zeros_like(accum)

    first = 0
    for hidden_ref, kl_ref, vl_ref, slots in zip(hidden_refs, kl_refs, vl_refs, groups):

        @pl.when((step >= first) & (step < first + len(slots)))
        def _():
            hidden = hidden_ref[...]
            accum[:, :k_width] += dot(hidden, kl_ref[...], 0, 0)
            accum[:, k_width:] += dot(hidden, vl_ref[...], 0, 0)

        first += len(slots)

    @pl.when(step == pl.num_programs(0) - 1)
    def _():
        keep[:model, q_width:] = accum[...]
        terms = jnp.sum(keep[:model, :q_width] * wq_ref[...].astype(F32), axis=1, keepdims=True)
        terms += jnp.sum(accum[:, :k_width] * wk_ref[...].astype(F32), axis=1, keepdims=True)
        terms += jnp.sum(accum[:, k_width:] * wv_ref[...].astype(F32), axis=1, keepdims=True)
        gain_grad_ref[...] = terms / gain_ref[...]
        rows = mine_ref.shape[0]
        core = core_ref[0]
        mine_ref[...] = keep[pl.ds(pl.multiple_of(core * rows, rows), rows), :].astype(BF)
        other_ref[...] = keep[pl.ds(pl.multiple_of((1 - core) * rows, rows), rows), :].astype(BF)


def split_kernel(place_ref, mine_ref, got_ref, *refs):
    rows = refs[0].shape[0]
    for k, ref in enumerate(refs):
        here = pl.ds(pl.multiple_of(place_ref[k] * rows, rows), rows)
        ref[...] = (mine_ref[here, :].astype(F32) + got_ref[here, :].astype(F32)).astype(ref.dtype)


def spread_kernel(q_width, k_width, model, *refs):
    place_ref = refs[0]
    *chunks, dq_ref, dk_ref, dv_ref, do_ref, full = refs[1:]
    rows = chunks[0].shape[0]
    for i, ref in enumerate(chunks):
        full[pl.ds(pl.multiple_of(place_ref[i] * rows, rows), rows), :] = ref[...].astype(F32)
    dq_ref[...] = full[:model, :q_width]
    dk_ref[...] = full[:model, q_width : q_width + k_width]
    dv_ref[...] = full[:model, q_width + k_width :]
    do_ref[...] = full[model:, :]


def slot_blocks(group, rows, width):
    first = group[0]
    gap = group[1] - group[0] if len(group) > 1 else 1
    return pl.BlockSpec((rows, width), lambda i: (first + gap * i, 0))


def on_device(
    tokens,
    norm1_gain,
    q_weight,
    key_matrix,
    value_matrix,
    q_gain,
    k_gain,
    o_weight,
    norm2_gain,
    gate_weight,
    up_weight,
    down_weight,
    out_grad,
    lengths,
    pairing,
):
    width = q_gain.shape[0]
    model = tokens.shape[2]
    share = tokens.shape[1]
    mp = lax.axis_size("mp")
    ctx = lax.axis_size("ctx")
    q_width = q_weight.shape[1]
    k_width = key_matrix.shape[1]
    kv_heads = k_width // width
    group_width = q_width // kv_heads
    feed = gate_weight.shape[1]
    ctx_rows = share * mp
    half = ctx_rows // 2
    seq_rows = ctx_rows * ctx
    few = ctx <= 4
    here_ctx = lax.axis_index("ctx")
    here_mp = lax.axis_index("mp")
    here_dp = lax.axis_index("dp")
    gain1 = norm1_gain.astype(F32)[None, :]
    gain2 = norm2_gain.astype(F32)[None, :]
    gq_col = q_gain.astype(F32)[:, None]
    gk_row = k_gain.astype(F32)[None, :]
    tok = tokens[0]
    og = out_grad[0]

    h1_share = call(norm_kernel, [tok, gain1], [out((share, model), BF)], name="norm1")[0]
    own_parts = [h1_share] + swaps([h1_share] * mp, "mp")
    if few:
        near = [from_ctx(h1_share, k) for k in range(1, ctx)]
        if ctx == 4:
            remote = [((1, 3), jnp.stack([near[0], near[2]])), ((2,), near[1][None])]
        else:
            remote = [(tuple(range(1, ctx)), jnp.stack(near))]
    else:
        every = lax.all_gather(h1_share, "ctx", axis=0)
        every = jnp.concatenate([every, every], axis=0)
        every = lax.dynamic_slice_in_dim(every, here_ctx + 1, ctx - 1, 0)
        remote = [(tuple(range(1, ctx)), every)]
    remote_parts = [[value] + swaps([value] * mp, "mp") for _, value in remote]
    groups = [(0,)] + [slots for slots, _ in remote]

    slot_ctx = (here_ctx + jnp.arange(ctx, dtype=jnp.int32)) % ctx
    slot_pair = jnp.sum(
        jnp.where(slot_ctx[:, None] == jnp.arange(ctx, dtype=jnp.int32)[None, :], pairing[None, :], 0),
        axis=1,
    )
    peers = here_mp ^ jnp.arange(mp, dtype=jnp.int32)
    rows_in = (peers[:, None] * share + jnp.arange(share, dtype=jnp.int32)[None, :]).reshape(-1)
    blocks = jnp.where(
        rows_in[None, :] < half, slot_pair[:, None], 2 * ctx - 1 - slot_pair[:, None]
    )
    positions = (blocks * half + (rows_in % half)[None, :]).reshape(-1)
    block_ids = blocks[:, ::half].reshape(-1)
    block_order = jnp.sum(
        jnp.where(
            block_ids[None, :] == jnp.arange(2 * ctx, dtype=jnp.int32)[:, None],
            jnp.arange(2 * ctx, dtype=jnp.int32)[None, :],
            0,
        ),
        axis=1,
    )
    last_block = block_ids[:2]
    own_pos = positions[:ctx_rows]
    doc_ends = jnp.cumsum(lengths[0])
    own_low = jnp.max(
        jnp.where(doc_ends[None, :] <= own_pos[:, None], doc_ends[None, :], 0), axis=1
    )
    qpos, qlow, kpos = own_pos[None, :], own_low[None, :], (rows_in % half)[:half, None]
    frequency = THETA ** (-(jnp.arange(width // 2, dtype=F32) * 2.0) / width)
    angles = positions.astype(F32)[:, None] * frequency[None, :]
    cos_half, sin_half = jnp.cos(angles), jnp.sin(angles)
    cosines = jnp.concatenate([cos_half, cos_half], axis=1)
    sines = jnp.concatenate([-sin_half, sin_half], axis=1)
    angles_t = frequency[:, None] * own_pos.astype(F32)[None, :]
    cos_t, sin_t = jnp.cos(angles_t), jnp.sin(angles_t)
    cosines_t = jnp.concatenate([cos_t, cos_t], axis=0)
    sines_t = jnp.concatenate([sin_t, sin_t], axis=0)

    qt, qlin, k_own, v_own, klin_own, h1_own = call(
        lambda *refs: own_kernel(mp, *refs),
        own_parts
        + [q_weight, key_matrix, value_matrix, gq_col, gk_row, cosines_t, sines_t, cosines, sines],
        [
            out((q_width, ctx_rows), BF),
            out((q_width, ctx_rows), F32),
            out((ctx_rows, k_width), BF),
            out((ctx_rows, k_width), BF),
            out((ctx_rows, k_width), F32),
            out((ctx_rows, model), BF),
        ],
        in_specs={
            mp + 7: pl.BlockSpec((ctx_rows, width), lambda i: (0, 0)),
            mp + 8: pl.BlockSpec((ctx_rows, width), lambda i: (0, 0)),
        },
        flops=2 * ctx_rows * model * (q_width + 2 * k_width),
        name="own_rows",
    )
    keys, values, klins, hiddens = [k_own], [v_own], [klin_own], [h1_own]
    for (slots, _), parts in zip(remote, remote_parts):
        size = len(slots)
        k_new, v_new, klin_new, h1_new = call(
            lambda *refs: remote_kernel(mp, *refs),
            parts + [key_matrix, value_matrix, gk_row, cosines, sines],
            [
                out((size * ctx_rows, k_width), BF),
                out((size * ctx_rows, k_width), BF),
                out((size * ctx_rows, k_width), F32),
                out((size * ctx_rows, model), BF),
            ],
            grid=(size,),
            in_specs={
                **{j: pl.BlockSpec((1, share, model), lambda i: (i, 0, 0)) for j in range(mp)},
                mp + 3: slot_blocks(slots, ctx_rows, width),
                mp + 4: slot_blocks(slots, ctx_rows, width),
            },
            out_specs={
                0: pl.BlockSpec((ctx_rows, k_width), lambda i: (i, 0)),
                1: pl.BlockSpec((ctx_rows, k_width), lambda i: (i, 0)),
                2: pl.BlockSpec((ctx_rows, k_width), lambda i: (i, 0)),
                3: pl.BlockSpec((ctx_rows, model), lambda i: (i, 0)),
            },
            flops=4 * size * ctx_rows * model * k_width,
            name="remote_rows",
        )
        keys.append(k_new)
        values.append(v_new)
        klins.append(klin_new)
        hiddens.append(h1_new)

    if few:
        joined, buffers = groups, {}
    else:
        joined = [tuple(range(ctx))]
        keys, values = [jnp.concatenate(keys, axis=0)], [jnp.concatenate(values, axis=0)]
        buffers = {"pipeline_mode": pl.Buffered(1)}
    by_head = [
        pl.BlockSpec((ctx_rows * len(slots), width), lambda h: (0, h), **buffers) for slots in joined
    ]
    n = len(joined)
    copies = [pltpu.VMEM((seq_rows if few else 16, width), BF)] * 2
    lanes = group_width // width * half
    t_block = pl.BlockSpec((group_width, ctx_rows), lambda h: (h, 0))
    wo_block = pl.BlockSpec((group_width, model), lambda h: (h, 0))
    sums_block = pl.BlockSpec((1, 2, lanes), lambda h: (h, 0, 0))
    pair_flops = 2 * q_width * ctx_rows * seq_rows
    ot, att_t, sums, *o_parts = call(
        lambda *refs: attend_kernel(joined, ctx_rows, width, mp, *refs),
        [block_order, last_block, kpos, qpos, qlow, qt, o_weight] + keys + values,
        [
            out((q_width, ctx_rows), F32),
            out((q_width, ctx_rows), BF),
            out((kv_heads, 2, lanes), F32),
            out((share, model), F32),
        ]
        + [out((share, model), BF)] * (mp - 1),
        grid=(kv_heads,),
        in_specs={
            0: SMEM,
            1: SMEM,
            5: t_block,
            6: wo_block,
            **{7 + i: by_head[i] for i in range(n)},
            **{7 + n + i: by_head[i] for i in range(n)},
        },
        out_specs={0: t_block, 1: t_block, 2: sums_block},
        scratch=copies
        + [
            pltpu.VMEM((width, lanes), F32),
            pltpu.VMEM((1, lanes), F32),
            pltpu.VMEM((ctx_rows, model), F32),
        ],
        flops=2 * pair_flops,
        name="attend",
    )
    resid, h2_share = call(
        resid_kernel,
        [tok, o_parts[0]] + swaps(o_parts, "mp") + [gain2],
        [out((share, model), F32), out((share, model), BF)],
        name="resid",
    )

    grad_full = lax.all_gather(og, "mp", axis=0, tiled=True)
    tile = 256 if feed % 256 == 0 else feed
    col_block = pl.BlockSpec((model, tile), lambda i: (0, i))
    row_block = pl.BlockSpec((tile, model), lambda i: (i, 0))
    act_block = pl.BlockSpec((ctx_rows, tile), lambda i: (0, i))
    h2_full, og_full, act, gate_grad, up_grad, *h2_parts = call(
        lambda *refs: feed_kernel(mp, *refs),
        [peers, h2_share]
        + swaps([h2_share] * mp, "mp")
        + [grad_full, gate_weight, up_weight, down_weight],
        [out((ctx_rows, model), BF)] * 2
        + [out((ctx_rows, feed), BF)] * 3
        + [out((share, model), F32)]
        + [out((share, model), BF)] * (mp - 1),
        grid=(feed // tile,),
        in_specs={0: SMEM, mp + 2: col_block, mp + 3: col_block, mp + 4: row_block},
        out_specs={2: act_block, 3: act_block, 4: act_block},
        scratch=[pltpu.VMEM((ctx_rows, model), F32)],
        flops=10 * ctx_rows * model * feed,
        name="feed",
    )
    h2_got = swaps(h2_parts, "mp")
    dg, du, dd, *f_parts = call(
        feed_weights_kernel,
        [h2_full, og_full, act, gate_grad, up_grad, down_weight],
        [out((model, feed), BF)] * 2
        + [out((feed, model), BF), out((share, model), F32)]
        + [out((share, model), BF)] * (mp - 1),
        grid=(feed // tile,),
        in_specs={2: act_block, 3: act_block, 4: act_block, 5: row_block},
        out_specs={0: col_block, 1: col_block, 2: row_block},
        scratch=[pltpu.VMEM((ctx_rows, model), F32)],
        flops=8 * ctx_rows * model * feed,
        name="feed_weights",
    )
    dg, du, dd = lax.psum((dg, du, dd), ("dp", "ctx"))

    resid_grad, low_share, gain2_part = call(
        resid_back_kernel,
        [resid, og, gain2, h2_parts[0]] + h2_got,
        [out((share, model), F32), out((share, model), BF), out((1, model), F32)],
        name="resid_back",
    )
    low_parts = [low_share] + swaps([low_share] * mp, "mp")

    head_rows = pl.BlockSpec((seq_rows, width), lambda h: (0, h), **buffers)
    ql, dk, dv, gq_part = call(
        lambda *refs: attend_back_kernel(joined, ctx_rows, width, mp, *refs),
        [block_order, last_block, kpos, qpos, qlow]
        + low_parts
        + [o_weight, qt, qlin, ot, sums, gq_col, cosines_t, sines_t]
        + keys
        + values,
        [
            out((q_width, ctx_rows), BF),
            out((seq_rows, k_width), F32),
            out((seq_rows, k_width), F32),
            out((width, 1), F32),
        ],
        grid=(kv_heads,),
        in_specs={
            0: SMEM,
            1: SMEM,
            5 + mp: wo_block,
            6 + mp: t_block,
            7 + mp: t_block,
            8 + mp: t_block,
            9 + mp: sums_block,
            **{13 + mp + m * n + i: by_head[i] for m in range(2) for i in range(n)},
        },
        out_specs={0: t_block, 1: head_rows, 2: head_rows},
        scratch=copies
        + [
            pltpu.VMEM((width, lanes), F32),
            pltpu.VMEM((ctx_rows, model), BF),
            pltpu.VMEM((group_width, ctx_rows), F32),
        ],
        flops=5 * pair_flops,
        name="attend_back",
    )

    f_got = swaps(f_parts, "mp")
    output = call(
        sum_kernel, [resid, f_parts[0]] + f_got, [out((share, model), BF)], name="output"
    )[0][None]

    lows = {}

    def hidden_back(slots):
        size = len(slots)
        own = slots == (0,)
        at = groups.index(slots)
        ins = ([ql, q_weight] if own else []) + [
            dk, dv, klins[at], cosines, sines, gk_row, key_matrix, value_matrix
        ]
        skip = 2 if own else 0
        block = slot_blocks(slots, ctx_rows, k_width)
        table = slot_blocks(slots, ctx_rows, width)
        here = pl.BlockSpec((ctx_rows, k_width), lambda i: (i, 0))
        kl, vl, gk_part, *parts = call(
            lambda *refs: hidden_back_kernel(own, mp, *refs),
            ins,
            [out((size * ctx_rows, k_width), BF)] * 2
            + [out((1, width), F32), out((size, share, model), F32)]
            + [out((size, share, model), BF)] * (mp - 1),
            grid=(size,),
            in_specs={skip: block, skip + 1: block, skip + 2: here, skip + 3: table, skip + 4: table},
            out_specs={
                0: here,
                1: here,
                **{3 + j: pl.BlockSpec((1, share, model), lambda i: (i, 0, 0)) for j in range(mp)},
            },
            flops=4 * size * ctx_rows * model * k_width,
            name="hidden_back",
        )
        lows[at] = (kl, vl, gk_part)
        return parts, swaps(parts, "mp")

    terms = []
    if few:
        for slots in ([(2,), (1, 3)] if ctx == 4 else [tuple(range(1, ctx))]):
            parts, got = hidden_back(slots)
            for i, slot in enumerate(slots):
                summed = sum_parts([p[i] for p in [parts[0]] + got], BF)
                terms.append(to_ctx(summed, slot))
    else:
        parts, got = hidden_back(tuple(range(1, ctx)))
        summed = (parts[0] + sum(p.astype(F32) for p in got)).astype(BF)
        padded = jnp.concatenate([jnp.zeros_like(summed[:1]), summed], axis=0)
        padded = jnp.concatenate([padded, padded], axis=0)
        natural = lax.dynamic_slice_in_dim(padded, (ctx - here_ctx) % ctx, ctx, 0)
        terms.append(lax.psum_scatter(natural, "ctx", scatter_dimension=0, tiled=False))
    parts, got = hidden_back((0,))
    terms = [p[0] for p in [parts[0]] + got] + terms
    input_grad = call(
        input_back_kernel, [tok, resid_grad, gain1] + terms, [out((share, model), F32)], name="input_back"
    )[0][None]

    total_rows = model + q_width
    kls, vls, gk_parts = zip(*[lows[i] for i in range(len(groups))])
    gk_part = sum(gk_parts[1:], gk_parts[0])
    m = len(groups)
    starts = [sum(len(slots) for slots in groups[:i]) for i in range(m)]

    def stepped(i, rows, columns):
        first, size = starts[i], len(groups[i])
        return pl.BlockSpec((rows, columns), lambda s: (jnp.clip(s - first, 0, size - 1), 0))

    mine, other, gain1_part = call(
        lambda *refs: weights_kernel(groups, mp, *refs),
        [here_dp[None], ql, att_t]
        + hiddens
        + list(kls)
        + list(vls)
        + low_parts
        + [q_weight, key_matrix, value_matrix, norm1_gain.astype(F32)[:, None]],
        [out((total_rows // 2, q_width + 2 * k_width), BF)] * 2 + [out((model, 1), F32)],
        grid=(ctx,),
        in_specs={
            0: SMEM,
            **{3 + i: stepped(i, ctx_rows, model) for i in range(m)},
            **{3 + m + i: stepped(i, ctx_rows, k_width) for i in range(m)},
            **{3 + 2 * m + i: stepped(i, ctx_rows, k_width) for i in range(m)},
        },
        scratch=[
            pltpu.VMEM((model, 2 * k_width), F32),
            pltpu.VMEM((ctx_rows, model), BF),
            pltpu.VMEM((total_rows, q_width + 2 * k_width), F32),
        ],
        flops=2 * model * (ctx_rows * q_width * 2 + 2 * seq_rows * k_width),
        name="weights",
    )
    got = swap(other, "dp", 1)
    if few:
        rows = total_rows // 2 // ctx
        places = slot_ctx
        pieces = call(
            split_kernel,
            [places, mine, got],
            [out((rows, mine.shape[1]), F32)] + [out((rows, mine.shape[1]), BF)] * (ctx - 1),
            in_specs={0: SMEM},
            name="split",
        )
        chunk = sum_parts(
            [pieces[0]] + [to_ctx(pieces[k], k) for k in range(1, ctx)], BF
        )
        chunks = [chunk] + [from_ctx(chunk, k) for k in range(1, ctx)]
        chunks = chunks + [swap(c, "dp", 1) for c in chunks]
        spots = jnp.concatenate([places + here_dp * ctx, places + (1 - here_dp) * ctx])
    else:
        chunk = lax.psum(sum_parts([mine, got], BF), "ctx")
        chunks = [chunk, swap(chunk, "dp", 1)]
        spots = jnp.stack([here_dp, 1 - here_dp])
    q_w_grad, k_w_grad, v_w_grad, o_w_grad = call(
        lambda *refs: spread_kernel(q_width, k_width, model, *refs),
        [spots] + chunks,
        [
            out((model, q_width), F32),
            out((model, k_width), F32),
            out((model, k_width), F32),
            out((q_width, model), F32),
        ],
        in_specs={0: SMEM},
        scratch=[pltpu.VMEM((total_rows, q_width + 2 * k_width), F32)],
        name="spread",
    )

    gains = jnp.concatenate(
        [gain1_part.reshape(-1), gain2_part.reshape(-1), gq_part.reshape(-1), gk_part.reshape(-1)]
    )
    if few:
        gains = gains + swap(gains, "dp", 1)
        gains = sum(swaps([gains] * mp, "mp"), gains)
        gains = sum([from_ctx(gains, k) for k in range(1, ctx)], gains)
    else:
        gains = lax.psum(gains, ("dp", "ctx", "mp"))
    return (
        output,
        input_grad,
        gains[:model],
        q_w_grad,
        k_w_grad,
        v_w_grad,
        gains[2 * model : 2 * model + width],
        gains[2 * model + width :],
        o_w_grad,
        gains[model : 2 * model],
        dg.astype(F32),
        du.astype(F32),
        dd.astype(F32),
    )


def solution(mesh):
    placed = (
        P("dp", ("ctx", "mp"), None),
        P(),
        P(None, "mp"),
        P(None, "mp"),
        P(None, "mp"),
        P(),
        P(),
        P("mp", None),
        P(),
        P(None, "mp"),
        P(None, "mp"),
        P("mp", None),
        P("dp", ("ctx", "mp"), None),
        P("dp", None),
        P(),
    )
    return jax.shard_map(
        on_device,
        mesh=mesh,
        in_specs=placed,
        out_specs=(
            P("dp", ("ctx", "mp"), None),
            P("dp", ("ctx", "mp"), None),
            P(),
            P(None, "mp"),
            P(None, "mp"),
            P(None, "mp"),
            P(),
            P(),
            P("mp", None),
            P(),
            P(None, "mp"),
            P(None, "mp"),
            P("mp", None),
        ),
        check_vma=False,
    )
```

```python
import math

import jax
import jax.numpy as jnp
from jax import lax
from jax.experimental import pallas as pl
from jax.experimental.pallas import tpu as pltpu
from jax.sharding import PartitionSpec as P

EPS = 1e-06
THETA = 1000000.0
LOG2E = 1.4426950408889634
BF = jnp.bfloat16
F32 = jnp.float32
VMEM_LIMIT = 52 * 1024 * 1024


def dot(left, right, left_dim, right_dim):
    return lax.dot_general(
        left, right, (((left_dim,), (right_dim,)), ((), ())), preferred_element_type=F32
    )


def whole_spec(array):
    rank = len(array.shape)
    return pl.BlockSpec(array.shape, lambda *_: (0,) * rank)


SMEM = pl.BlockSpec(memory_space=pltpu.SMEM)


def call(kernel, ins, outs, grid=(1,), in_specs=None, out_specs=None, scratch=(), flops=0, name=None):
    in_specs = in_specs or {}
    out_specs = out_specs or {}
    return pl.pallas_call(
        kernel,
        grid=grid,
        in_specs=[in_specs.get(i, whole_spec(a)) for i, a in enumerate(ins)],
        out_specs=[out_specs.get(i, whole_spec(a)) for i, a in enumerate(outs)],
        out_shape=list(outs),
        scratch_shapes=list(scratch),
        compiler_params=pltpu.CompilerParams(vmem_limit_bytes=VMEM_LIMIT),
        cost_estimate=pl.CostEstimate(flops=0, bytes_accessed=0, transcendentals=0),
        name=name,
    )(*ins)


def out(shape, dtype):
    return jax.ShapeDtypeStruct(shape, dtype)


def swap(value, axis, step):
    size = lax.axis_size(axis)
    return lax.ppermute(value, axis, [(i, i ^ step) for i in range(size)])


def swaps(values, axis):
    order = sorted(range(1, len(values)), key=lambda j: -bin(j).count("1"))
    got = {j: swap(values[j], axis, j) for j in order}
    return [got[j] for j in range(1, len(values))]


def from_ctx(value, step):
    size = lax.axis_size("ctx")
    return lax.ppermute(value, "ctx", [((i + step) % size, i) for i in range(size)])


def to_ctx(value, step):
    size = lax.axis_size("ctx")
    return lax.ppermute(value, "ctx", [(i, (i + step) % size) for i in range(size)])


def norm_kernel(rows_ref, gain_ref, normed_ref):
    rows = rows_ref[...].astype(F32)
    factor = lax.rsqrt(jnp.mean(rows * rows, axis=-1, keepdims=True) + EPS)
    normed_ref[...] = (rows * factor * gain_ref[...]).astype(BF)


def resid_kernel(tok_ref, own_ref, *refs):
    *parts, gain_ref, resid_ref, normed_ref = refs
    rows = tok_ref[...].astype(F32) + own_ref[...]
    for part in parts:
        rows = rows + part[...].astype(F32)
    resid_ref[...] = rows
    factor = lax.rsqrt(jnp.mean(rows * rows, axis=-1, keepdims=True) + EPS)
    normed_ref[...] = (rows * factor * gain_ref[...]).astype(BF)


def norm_back(rows, gain, gradient):
    factor = lax.rsqrt(jnp.mean(rows * rows, axis=-1, keepdims=True) + EPS)
    scaled = gradient * gain
    inner = jnp.mean(scaled * rows, axis=-1, keepdims=True)
    return factor * scaled - rows * (factor * factor * factor) * inner, gradient * rows * factor


def resid_back_kernel(resid_ref, grad_ref, gain_ref, own_ref, *refs):
    *parts, full_ref, low_ref, gain_grad_ref = refs
    gradient = own_ref[...]
    for part in parts:
        gradient = gradient + part[...].astype(F32)
    back, terms = norm_back(resid_ref[...], gain_ref[...], gradient)
    total = grad_ref[...].astype(F32) + back
    full_ref[...] = total
    low_ref[...] = total.astype(BF)
    gain_grad_ref[...] = jnp.sum(terms, axis=0, keepdims=True)


def input_back_kernel(tok_ref, resid_grad_ref, gain_ref, *refs):
    *parts, result_ref = refs
    gradient = parts[0][...].astype(F32)
    for part in parts[1:]:
        gradient = gradient + part[...].astype(F32)
    back, _ = norm_back(tok_ref[...].astype(F32), gain_ref[...], gradient)
    result_ref[...] = resid_grad_ref[...] + back


def sum_kernel(*refs):
    *parts, result_ref = refs
    total = parts[0][...].astype(F32)
    for part in parts[1:]:
        total = total + part[...].astype(F32)
    result_ref[...] = total.astype(result_ref.dtype)


def sum_parts(parts, dtype):
    return call(sum_kernel, parts, [out(parts[0].shape, dtype)], name="sum_parts")[0]


def key_rows(linear, gain, cosines, sines):
    heads = []
    for start in range(0, linear.shape[1], gain.shape[1]):
        rows = linear[:, start : start + gain.shape[1]]
        factor = lax.rsqrt(jnp.mean(rows * rows, axis=-1, keepdims=True) + EPS)
        normed = rows * factor * gain
        turned = pltpu.roll(normed, normed.shape[1] // 2, 1)
        heads.append((normed * cosines + turned * sines).astype(BF))
    return heads


def key_value_part(hidden, wk_ref, wv_ref, gk_ref, cos_ref, sin_ref, k_ref, v_ref, klin_ref):
    linear = dot(hidden, wk_ref[...], 1, 0)
    klin_ref[...] = linear
    width = gk_ref.shape[1]
    for head, rows in enumerate(key_rows(linear, gk_ref[...], cos_ref[...], sin_ref[...])):
        k_ref[:, head * width : (head + 1) * width] = rows
    v_ref[...] = dot(hidden, wv_ref[...], 1, 0).astype(BF)


def turn_rows(value):
    half = value.shape[0] // 2
    return jnp.concatenate([-value[half:], value[:half]], axis=0)


def own_kernel(count, *refs):
    parts = refs[:count]
    (wq_ref, wk_ref, wv_ref, gq_ref, gk_ref, cos_t_ref, sin_t_ref, cos_ref, sin_ref) = refs[
        count : count + 9
    ]
    qt_ref, qlin_ref, k_ref, v_ref, klin_ref, hidden_ref = refs[count + 9 :]
    share = parts[0].shape[0]
    for j, part in enumerate(parts):
        hidden_ref[j * share : (j + 1) * share, :] = part[...]
    hidden = hidden_ref[...]
    key_value_part(hidden, wk_ref, wv_ref, gk_ref, cos_ref, sin_ref, k_ref, v_ref, klin_ref)
    linear = dot(wq_ref[...], hidden, 0, 1)
    qlin_ref[...] = linear
    width = gq_ref.shape[0]
    for start in range(0, linear.shape[0], width):
        rows = linear[start : start + width]
        factor = lax.rsqrt(jnp.mean(rows * rows, axis=0, keepdims=True) + EPS)
        normed = rows * factor * gq_ref[...]
        qt_ref[start : start + width, :] = (
            normed * cos_t_ref[...] + turn_rows(normed) * sin_t_ref[...]
        ).astype(BF)


def remote_kernel(count, *refs):
    parts = refs[:count]
    wk_ref, wv_ref, gk_ref, cos_ref, sin_ref = refs[count : count + 5]
    k_ref, v_ref, klin_ref, hidden_ref = refs[count + 5 :]
    share = parts[0].shape[1]
    for j, part in enumerate(parts):
        hidden_ref[j * share : (j + 1) * share, :] = part[0]
    key_value_part(
        hidden_ref[...], wk_ref, wv_ref, gk_ref, cos_ref, sin_ref, k_ref, v_ref, klin_ref
    )


def place_slots(target_ref, refs, groups, rows):
    if len(refs) == 1:
        return refs[0]
    for ref, group in zip(refs, groups):
        for i, slot in enumerate(group):
            target_ref[pl.ds(slot * rows, rows), :] = ref[i * rows : (i + 1) * rows, :]
    return target_ref


def lanes_of(ref, half_index, half, width):
    heads = [
        ref[start : start + width, half_index * half : (half_index + 1) * half]
        for start in range(0, ref.shape[0], width)
    ]
    return jnp.concatenate(heads, axis=1)


def attend_kernel(groups, ctx_rows, width, mp, *refs):
    n = len(groups)
    order_ref, last_ref, kpos_ref, qpos_ref, qlow_ref, qt_ref, wo_ref = refs[:7]
    k_refs, v_refs = refs[7 : 7 + n], refs[7 + n : 7 + 2 * n]
    rest = refs[7 + 2 * n :]
    ot_ref, attt_ref, sums_ref = rest[:3]
    part_refs = rest[3 : 3 + mp]
    k_all, v_all, numer, sums, projected = rest[3 + mp :]
    half = ctx_rows // 2
    share = ctx_rows // mp
    per_group = qt_ref.shape[0] // width
    k_all = place_slots(k_all, k_refs, groups, ctx_rows)
    v_all = place_slots(v_all, v_refs, groups, ctx_rows)
    scale = LOG2E / math.sqrt(width)
    for t in range(2):
        queries = lanes_of(qt_ref, t, half, width)
        qpos = jnp.concatenate([qpos_ref[:, t * half : (t + 1) * half]] * per_group, axis=1)
        qlow = jnp.concatenate([qlow_ref[:, t * half : (t + 1) * half]] * per_group, axis=1)
        numer[...] = jnp.zeros_like(numer)
        sums[...] = jnp.zeros_like(sums)

        def step(i, carry):
            start = pl.multiple_of(order_ref[i] * half, half)
            scores = dot(k_all[pl.ds(start, half), :], queries, 1, 0)
            kpos = kpos_ref[...] + i * half
            seen = (kpos <= qpos) & (kpos >= qlow)
            weights = jnp.where(seen, jnp.exp2(scores * scale), 0.0)
            sums[...] += jnp.sum(weights, axis=0, keepdims=True)
            numer[...] += dot(v_all[pl.ds(start, half), :], weights.astype(BF), 0, 0)
            return carry

        lax.fori_loop(0, last_ref[t] + 1, step, 0)
        total = sums[...]
        sums_ref[0, t : t + 1, :] = total
        result = numer[...] / total
        for head in range(per_group):
            piece = result[:, head * half : (head + 1) * half]
            ot_ref[head * width : (head + 1) * width, t * half : (t + 1) * half] = piece
            attt_ref[head * width : (head + 1) * width, t * half : (t + 1) * half] = piece.astype(BF)
    added = dot(attt_ref[...], wo_ref[...], 0, 0)
    group = pl.program_id(0)

    @pl.when(group == 0)
    def _():
        projected[...] = added

    @pl.when(group > 0)
    def _():
        projected[...] += added

    @pl.when(group == pl.num_programs(0) - 1)
    def _():
        for j, ref in enumerate(part_refs):
            ref[...] = projected[j * share : (j + 1) * share, :].astype(ref.dtype)


def feed_kernel(count, *refs):
    peer_ref = refs[0]
    parts = refs[1 : 1 + count]
    grad_ref, wg_ref, wu_ref, wd_ref = refs[1 + count : 5 + count]
    hidden_ref, grads_ref, act_ref, gg_ref, ug_ref = refs[5 + count : 10 + count]
    part_refs = refs[10 + count : 10 + 2 * count]
    total = refs[10 + 2 * count]
    share = parts[0].shape[0]
    step = pl.program_id(0)

    @pl.when(step == 0)
    def _():
        for j, part in enumerate(parts):
            hidden_ref[j * share : (j + 1) * share, :] = part[...]
            place = pl.multiple_of(peer_ref[j] * share, share)
            grads_ref[j * share : (j + 1) * share, :] = grad_ref[pl.ds(place, share), :]

    hidden = hidden_ref[...]
    gate = dot(hidden, wg_ref[...], 1, 0)
    up = dot(hidden, wu_ref[...], 1, 0)
    act_grad = dot(grads_ref[...], wd_ref[...], 1, 1)
    sig = 1.0 / (1.0 + jnp.exp(-gate))
    silu = gate * sig
    act_ref[...] = (silu * up).astype(BF)
    gate_grad = (act_grad * up * sig * (1.0 + gate * (1.0 - sig))).astype(BF)
    up_grad = (act_grad * silu).astype(BF)
    gg_ref[...] = gate_grad
    ug_ref[...] = up_grad
    added = dot(gate_grad, wg_ref[...], 1, 1) + dot(up_grad, wu_ref[...], 1, 1)

    @pl.when(step == 0)
    def _():
        total[...] = added

    @pl.when(step > 0)
    def _():
        total[...] += added

    @pl.when(step == pl.num_programs(0) - 1)
    def _():
        for j, ref in enumerate(part_refs):
            ref[...] = total[j * share : (j + 1) * share, :].astype(ref.dtype)


def feed_weights_kernel(hidden_ref, grads_ref, act_ref, gg_ref, ug_ref, wd_ref, *refs):
    dg_ref, du_ref, dd_ref = refs[:3]
    *part_refs, total = refs[3:]
    share = part_refs[0].shape[0]
    step = pl.program_id(0)
    dg_ref[...] = dot(hidden_ref[...], gg_ref[...], 0, 0).astype(BF)
    du_ref[...] = dot(hidden_ref[...], ug_ref[...], 0, 0).astype(BF)
    dd_ref[...] = dot(act_ref[...], grads_ref[...], 0, 0).astype(BF)
    added = dot(act_ref[...], wd_ref[...], 1, 0)

    @pl.when(step == 0)
    def _():
        total[...] = added

    @pl.when(step > 0)
    def _():
        total[...] += added

    @pl.when(step == pl.num_programs(0) - 1)
    def _():
        for j, ref in enumerate(part_refs):
            ref[...] = total[j * share : (j + 1) * share, :].astype(ref.dtype)


def attend_back_kernel(groups, ctx_rows, width, mp, *refs):
    n = len(groups)
    order_ref, last_ref, kpos_ref, qpos_ref, qlow_ref = refs[:5]
    low_refs = refs[5 : 5 + mp]
    wo_ref, qt_ref, qlin_ref, ot_ref, sums_ref, gq_ref, cos_t_ref, sin_t_ref = refs[
        5 + mp : 13 + mp
    ]
    at = 13 + mp
    k_refs, v_refs = refs[at : at + n], refs[at + n : at + 2 * n]
    at += 2 * n
    ql_ref, dk, dv, gqg_ref = refs[at : at + 4]
    k_all, v_all, dq, low_all, dqt = refs[at + 4 :]
    half = ctx_rows // 2
    share = ctx_rows // mp
    per_group = qt_ref.shape[0] // width
    scale = LOG2E / math.sqrt(width)
    score_scale = 1.0 / math.sqrt(width)
    group = pl.program_id(0)
    k_all = place_slots(k_all, k_refs, groups, ctx_rows)
    v_all = place_slots(v_all, v_refs, groups, ctx_rows)
    dk[...] = jnp.zeros_like(dk)
    dv[...] = jnp.zeros_like(dv)

    @pl.when(group == 0)
    def _():
        for j, ref in enumerate(low_refs):
            low_all[j * share : (j + 1) * share, :] = ref[...]
        gqg_ref[...] = jnp.zeros_like(gqg_ref)

    att_grad = dot(wo_ref[...], low_all[...], 1, 1).astype(BF).astype(F32)
    for t in range(2):
        queries = lanes_of(qt_ref, t, half, width)
        pre = lanes_of(ot_ref, t, half, width)
        grads = jnp.concatenate(
            [
                att_grad[h * width : (h + 1) * width, t * half : (t + 1) * half]
                for h in range(per_group)
            ],
            axis=1,
        )
        inverse = 1.0 / sums_ref[0, t : t + 1, :]
        scaled = (grads * inverse).astype(BF)
        shift = jnp.sum(grads * pre, axis=0, keepdims=True) * inverse
        qpos = jnp.concatenate([qpos_ref[:, t * half : (t + 1) * half]] * per_group, axis=1)
        qlow = jnp.concatenate([qlow_ref[:, t * half : (t + 1) * half]] * per_group, axis=1)
        dq[...] = jnp.zeros_like(dq)

        def step(i, carry):
            start = pl.multiple_of(order_ref[i] * half, half)
            keys = k_all[pl.ds(start, half), :]
            scores = dot(keys, queries, 1, 0)
            prob_grad = dot(v_all[pl.ds(start, half), :], scaled, 1, 0)
            kpos = kpos_ref[...] + i * half
            seen = (kpos <= qpos) & (kpos >= qlow)
            weights = jnp.where(seen, jnp.exp2(scores * scale), 0.0)
            score_grad = (weights * (prob_grad - shift)).astype(BF)
            dv[pl.ds(start, half), :] += dot(weights.astype(BF), scaled, 1, 1)
            dk[pl.ds(start, half), :] += dot(score_grad, queries, 1, 1)
            dq[...] += dot(keys, score_grad, 0, 0)
            return carry

        lax.fori_loop(0, last_ref[t] + 1, step, 0)
        for head in range(per_group):
            dqt[head * width : (head + 1) * width, t * half : (t + 1) * half] = dq[
                :, head * half : (head + 1) * half
            ]
    for head in range(per_group):
        rows = qlin_ref[head * width : (head + 1) * width, :]
        rotated = dqt[head * width : (head + 1) * width, :] * score_scale
        gradient = rotated * cos_t_ref[...] - turn_rows(rotated) * sin_t_ref[...]
        factor = lax.rsqrt(jnp.mean(rows * rows, axis=0, keepdims=True) + EPS)
        gained = gradient * gq_ref[...]
        inner = jnp.mean(gained * rows, axis=0, keepdims=True)
        ql_ref[head * width : (head + 1) * width, :] = (
            factor * gained - rows * (factor * factor * factor) * inner
        ).astype(BF)
        gqg_ref[...] += jnp.sum(gradient * rows * factor, axis=1, keepdims=True)


def hidden_back_kernel(own, mp, *refs):
    if own:
        ql_ref, wq_ref, *refs = refs
    kl_ref, vl_ref, wk_ref, wv_ref = refs[:4]
    part_refs = refs[4:]
    share = part_refs[0].shape[1]
    total = dot(kl_ref[...], wk_ref[...], 1, 1) + dot(vl_ref[...], wv_ref[...], 1, 1)
    if own:
        total = total + dot(ql_ref[...], wq_ref[...], 0, 1)
    for j, ref in enumerate(part_refs):
        ref[0] = total[j * share : (j + 1) * share, :].astype(ref.dtype)


def o_weights_kernel(core_ref, attt_ref, *refs):
    *low_refs, mine_ref, other_ref, low_all = refs
    share = low_refs[0].shape[0]
    for j, ref in enumerate(low_refs):
        low_all[j * share : (j + 1) * share, :] = ref[...]
    rows = mine_ref.shape[0]
    core = core_ref[0]
    for ref, at in ((mine_ref, core), (other_ref, 1 - core)):
        here = pl.ds(pl.multiple_of(at * rows, rows), rows)
        ref[...] = dot(attt_ref[here, :], low_all[...], 1, 0).astype(BF)


def weights_kernel(groups, *refs):
    n = len(groups)
    core_ref, ql_ref, dk_ref, dv_ref, cos_ref, sin_ref, gk_ref = refs[:7]
    hidden_refs, klin_refs = refs[7 : 7 + n], refs[7 + n : 7 + 2 * n]
    (
        wq_ref, wk_ref, wv_ref, gain_ref, kl_ref, vl_ref,
        mine_ref, other_ref, gain_grad_ref, gkg_ref, accum,
    ) = refs[7 + 2 * n :]
    step = pl.program_id(0)
    model = gain_ref.shape[0]
    q_width, k_width = ql_ref.shape[0], dk_ref.shape[1]
    width = gk_ref.shape[1]
    score_scale = 1.0 / math.sqrt(width)

    @pl.when(step == 0)
    def _():
        accum[:, :q_width] = dot(hidden_refs[0][...], ql_ref[...], 0, 1)
        accum[:, q_width:] = jnp.zeros_like(accum[:, q_width:])
        gkg_ref[...] = jnp.zeros_like(gkg_ref)

    first = 0
    for hidden_ref, klin_ref, slots in zip(hidden_refs, klin_refs, groups):

        @pl.when((step >= first) & (step < first + len(slots)))
        def _():
            for start in range(0, k_width, width):
                head = slice(start, start + width)
                rotated = dk_ref[:, head] * score_scale
                gradient = rotated * cos_ref[...] - pltpu.roll(rotated, width // 2, 1) * sin_ref[...]
                back, terms = norm_back(klin_ref[:, head], gk_ref[...], gradient)
                kl_ref[:, head] = back.astype(BF)
                gkg_ref[...] += jnp.sum(terms, axis=0, keepdims=True)
            vl_ref[...] = dv_ref[...].astype(BF)
            hidden = hidden_ref[...]
            accum[:, q_width : q_width + k_width] += dot(hidden, kl_ref[...], 0, 0)
            accum[:, q_width + k_width :] += dot(hidden, vl_ref[...], 0, 0)

        first += len(slots)

    @pl.when(step == pl.num_programs(0) - 1)
    def _():
        terms = jnp.sum(accum[:, :q_width] * wq_ref[...].astype(F32), axis=1, keepdims=True)
        terms += jnp.sum(
            accum[:, q_width : q_width + k_width] * wk_ref[...].astype(F32), axis=1, keepdims=True
        )
        terms += jnp.sum(
            accum[:, q_width + k_width :] * wv_ref[...].astype(F32), axis=1, keepdims=True
        )
        gain_grad_ref[...] = terms / gain_ref[...]
        rows = mine_ref.shape[0]
        core = core_ref[0]
        mine_ref[...] = accum[pl.ds(pl.multiple_of(core * rows, rows), rows), :].astype(BF)
        other_ref[...] = accum[pl.ds(pl.multiple_of((1 - core) * rows, rows), rows), :].astype(BF)


def split_kernel(place_ref, mine_ref, got_ref, keep_ref, send_ref):
    rows = keep_ref.shape[0]
    for ref, at in ((keep_ref, place_ref[0]), (send_ref, 1 - place_ref[0])):
        here = pl.ds(pl.multiple_of(at * rows, rows), rows)
        ref[...] = (mine_ref[here, :].astype(F32) + got_ref[here, :].astype(F32)).astype(ref.dtype)


def spread_kernel(q_width, k_width, count, *refs):
    place_ref = refs[0]
    chunks, o_chunks = refs[1 : 1 + count], refs[1 + count : 1 + 2 * count]
    dq_ref, dk_ref, dv_ref, do_ref = refs[1 + 2 * count :]
    for i, ref in enumerate(chunks):
        rows = ref.shape[0]
        here = pl.ds(pl.multiple_of(place_ref[i] * rows, rows), rows)
        dq_ref[here, :] = ref[:, :q_width].astype(F32)
        dk_ref[here, :] = ref[:, q_width : q_width + k_width].astype(F32)
        dv_ref[here, :] = ref[:, q_width + k_width :].astype(F32)
    for i, ref in enumerate(o_chunks):
        rows = ref.shape[0]
        here = pl.ds(pl.multiple_of(place_ref[i] * rows, rows), rows)
        do_ref[here, :] = ref[...].astype(F32)


def sum_over_ctx(mine, other, part, few, after=()):
    got = swap(other, "dp", 1)
    if not few:
        chunk = lax.psum(sum_parts([mine, got], BF), "ctx")
        return [chunk, swap(chunk, "dp", 1)]
    rows = mine.shape[0] // 2
    keep, send = call(
        split_kernel,
        [part, mine, got],
        [out((rows, mine.shape[1]), F32), out((rows, mine.shape[1]), BF)],
        in_specs={0: SMEM},
        name="split",
    )
    pair = sum_parts([keep, swap(send, "ctx", 1)], BF)
    if after:
        pair, *_ = lax.optimization_barrier((pair, *after))
    total = sum_parts([pair, swap(pair, "ctx", 3)], BF)
    chunks = [total, swap(total, "ctx", 1)]
    return chunks + [swap(c, "dp", 1) for c in chunks]


def slot_blocks(group, rows, width):
    first = group[0]
    gap = group[1] - group[0] if len(group) > 1 else 1
    return pl.BlockSpec((rows, width), lambda i: (first + gap * i, 0))


def on_device(
    tokens,
    norm1_gain,
    q_weight,
    key_matrix,
    value_matrix,
    q_gain,
    k_gain,
    o_weight,
    norm2_gain,
    gate_weight,
    up_weight,
    down_weight,
    out_grad,
    lengths,
    pairing,
):
    width = q_gain.shape[0]
    model = tokens.shape[2]
    share = tokens.shape[1]
    mp = lax.axis_size("mp")
    ctx = lax.axis_size("ctx")
    q_width = q_weight.shape[1]
    k_width = key_matrix.shape[1]
    kv_heads = k_width // width
    group_width = q_width // kv_heads
    feed = gate_weight.shape[1]
    ctx_rows = share * mp
    half = ctx_rows // 2
    seq_rows = ctx_rows * ctx
    few = ctx == 4
    here_ctx = lax.axis_index("ctx")
    here_mp = lax.axis_index("mp")
    here_dp = lax.axis_index("dp")
    gain1 = norm1_gain.astype(F32)[None, :]
    gain2 = norm2_gain.astype(F32)[None, :]
    gq_col = q_gain.astype(F32)[:, None]
    gk_row = k_gain.astype(F32)[None, :]
    tok = tokens[0]
    og = out_grad[0]

    h1_share = call(norm_kernel, [tok, gain1], [out((share, model), BF)], name="norm1")[0]
    own_parts = [h1_share] + swaps([h1_share] * mp, "mp")
    if few:
        near = {k: from_ctx(h1_share, k) for k in (1, 3)}
        own_parts[0], near[1], near[3] = lax.optimization_barrier((own_parts[0], near[1], near[3]))

    slot_ctx = (here_ctx + jnp.arange(ctx, dtype=jnp.int32)) % ctx
    slot_pair = jnp.sum(
        jnp.where(slot_ctx[:, None] == jnp.arange(ctx, dtype=jnp.int32)[None, :], pairing[None, :], 0),
        axis=1,
    )
    peers = here_mp ^ jnp.arange(mp, dtype=jnp.int32)
    rows_in = (peers[:, None] * share + jnp.arange(share, dtype=jnp.int32)[None, :]).reshape(-1)
    blocks = jnp.where(
        rows_in[None, :] < half, slot_pair[:, None], 2 * ctx - 1 - slot_pair[:, None]
    )
    positions = (blocks * half + (rows_in % half)[None, :]).reshape(-1)
    block_ids = blocks[:, ::half].reshape(-1)
    block_order = jnp.sum(
        jnp.where(
            block_ids[None, :] == jnp.arange(2 * ctx, dtype=jnp.int32)[:, None],
            jnp.arange(2 * ctx, dtype=jnp.int32)[None, :],
            0,
        ),
        axis=1,
    )
    last_block = block_ids[:2]
    own_pos = positions[:ctx_rows]
    doc_ends = jnp.cumsum(lengths[0])
    own_low = jnp.max(
        jnp.where(doc_ends[None, :] <= own_pos[:, None], doc_ends[None, :], 0), axis=1
    )
    qpos, qlow, kpos = own_pos[None, :], own_low[None, :], (rows_in % half)[:half, None]
    frequency = THETA ** (-(jnp.arange(width // 2, dtype=F32) * 2.0) / width)
    angles = positions.astype(F32)[:, None] * frequency[None, :]
    cos_half, sin_half = jnp.cos(angles), jnp.sin(angles)
    cosines = jnp.concatenate([cos_half, cos_half], axis=1)
    sines = jnp.concatenate([-sin_half, sin_half], axis=1)
    angles_t = frequency[:, None] * own_pos.astype(F32)[None, :]
    cos_t, sin_t = jnp.cos(angles_t), jnp.sin(angles_t)
    cosines_t = jnp.concatenate([cos_t, cos_t], axis=0)
    sines_t = jnp.concatenate([sin_t, sin_t], axis=0)

    qt, qlin, k_own, v_own, klin_own, h1_own = call(
        lambda *refs: own_kernel(mp, *refs),
        own_parts
        + [q_weight, key_matrix, value_matrix, gq_col, gk_row, cosines_t, sines_t, cosines, sines],
        [
            out((q_width, ctx_rows), BF),
            out((q_width, ctx_rows), F32),
            out((ctx_rows, k_width), BF),
            out((ctx_rows, k_width), BF),
            out((ctx_rows, k_width), F32),
            out((ctx_rows, model), BF),
        ],
        in_specs={
            mp + 7: pl.BlockSpec((ctx_rows, width), lambda i: (0, 0)),
            mp + 8: pl.BlockSpec((ctx_rows, width), lambda i: (0, 0)),
        },
        flops=2 * ctx_rows * model * (q_width + 2 * k_width),
        name="own_rows",
    )
    if few:
        late_share, _ = lax.optimization_barrier((h1_share, k_own))
        far = from_ctx(late_share, 2)
        remote = [((1, 3), jnp.stack([near[1], near[3]])), ((2,), far[None])]
    else:
        every = lax.all_gather(h1_share, "ctx", axis=0)
        every = jnp.concatenate([every, every], axis=0)
        every = lax.dynamic_slice_in_dim(every, here_ctx + 1, ctx - 1, 0)
        remote = [(tuple(range(1, ctx)), every)]
    remote_parts = [[value] + swaps([value] * mp, "mp") for _, value in remote]
    groups = [(0,)] + [slots for slots, _ in remote]
    keys, values, klins, hiddens = [k_own], [v_own], [klin_own], [h1_own]
    for (slots, _), parts in zip(remote, remote_parts):
        size = len(slots)
        k_new, v_new, klin_new, h1_new = call(
            lambda *refs: remote_kernel(mp, *refs),
            parts + [key_matrix, value_matrix, gk_row, cosines, sines],
            [
                out((size * ctx_rows, k_width), BF),
                out((size * ctx_rows, k_width), BF),
                out((size * ctx_rows, k_width), F32),
                out((size * ctx_rows, model), BF),
            ],
            grid=(size,),
            in_specs={
                **{j: pl.BlockSpec((1, share, model), lambda i: (i, 0, 0)) for j in range(mp)},
                mp + 3: slot_blocks(slots, ctx_rows, width),
                mp + 4: slot_blocks(slots, ctx_rows, width),
            },
            out_specs={
                0: pl.BlockSpec((ctx_rows, k_width), lambda i: (i, 0)),
                1: pl.BlockSpec((ctx_rows, k_width), lambda i: (i, 0)),
                2: pl.BlockSpec((ctx_rows, k_width), lambda i: (i, 0)),
                3: pl.BlockSpec((ctx_rows, model), lambda i: (i, 0)),
            },
            flops=4 * size * ctx_rows * model * k_width,
            name="remote_rows",
        )
        keys.append(k_new)
        values.append(v_new)
        klins.append(klin_new)
        hiddens.append(h1_new)

    if few:
        joined, buffers = groups, {}
    else:
        joined = [tuple(range(ctx))]
        keys, values = [jnp.concatenate(keys, axis=0)], [jnp.concatenate(values, axis=0)]
        buffers = {"pipeline_mode": pl.Buffered(1)}
    by_head = [
        pl.BlockSpec((ctx_rows * len(slots), width), lambda h: (0, h), **buffers) for slots in joined
    ]
    n = len(joined)
    copies = [pltpu.VMEM((seq_rows if few else 16, width), BF)] * 2
    lanes = group_width // width * half
    t_block = pl.BlockSpec((group_width, ctx_rows), lambda h: (h, 0))
    wo_block = pl.BlockSpec((group_width, model), lambda h: (h, 0))
    sums_block = pl.BlockSpec((1, 2, lanes), lambda h: (h, 0, 0))
    pair_flops = 2 * q_width * ctx_rows * seq_rows
    ot, att_t, sums, *o_parts = call(
        lambda *refs: attend_kernel(joined, ctx_rows, width, mp, *refs),
        [block_order, last_block, kpos, qpos, qlow, qt, o_weight] + keys + values,
        [
            out((q_width, ctx_rows), F32),
            out((q_width, ctx_rows), BF),
            out((kv_heads, 2, lanes), F32),
            out((share, model), F32),
        ]
        + [out((share, model), BF)] * (mp - 1),
        grid=(kv_heads,),
        in_specs={
            0: SMEM,
            1: SMEM,
            5: t_block,
            6: wo_block,
            **{7 + i: by_head[i] for i in range(n)},
            **{7 + n + i: by_head[i] for i in range(n)},
        },
        out_specs={0: t_block, 1: t_block, 2: sums_block},
        scratch=copies
        + [
            pltpu.VMEM((width, lanes), F32),
            pltpu.VMEM((1, lanes), F32),
            pltpu.VMEM((ctx_rows, model), F32),
        ],
        flops=2 * pair_flops,
        name="attend",
    )
    resid, h2_share = call(
        resid_kernel,
        [tok, o_parts[0]] + swaps(o_parts, "mp") + [gain2],
        [out((share, model), F32), out((share, model), BF)],
        name="resid",
    )

    og_late, *_ = lax.optimization_barrier((og, *[parts[-1] for parts in remote_parts]))
    grad_full = lax.all_gather(og_late, "mp", axis=0, tiled=True)
    tile = 256 if feed % 256 == 0 else feed
    col_block = pl.BlockSpec((model, tile), lambda i: (0, i))
    row_block = pl.BlockSpec((tile, model), lambda i: (i, 0))
    act_block = pl.BlockSpec((ctx_rows, tile), lambda i: (0, i))
    h2_full, og_full, act, gate_grad, up_grad, *h2_parts = call(
        lambda *refs: feed_kernel(mp, *refs),
        [peers, h2_share]
        + swaps([h2_share] * mp, "mp")
        + [grad_full, gate_weight, up_weight, down_weight],
        [out((ctx_rows, model), BF)] * 2
        + [out((ctx_rows, feed), BF)] * 3
        + [out((share, model), F32)]
        + [out((share, model), BF)] * (mp - 1),
        grid=(feed // tile,),
        in_specs={0: SMEM, mp + 2: col_block, mp + 3: col_block, mp + 4: row_block},
        out_specs={2: act_block, 3: act_block, 4: act_block},
        scratch=[pltpu.VMEM((ctx_rows, model), F32)],
        flops=10 * ctx_rows * model * feed,
        name="feed",
    )
    h2_got = swaps(h2_parts, "mp")
    dg, du, dd, *f_parts = call(
        feed_weights_kernel,
        [h2_full, og_full, act, gate_grad, up_grad, down_weight],
        [out((model, feed), BF)] * 2
        + [out((feed, model), BF), out((share, model), F32)]
        + [out((share, model), BF)] * (mp - 1),
        grid=(feed // tile,),
        in_specs={2: act_block, 3: act_block, 4: act_block, 5: row_block},
        out_specs={0: col_block, 1: col_block, 2: row_block},
        scratch=[pltpu.VMEM((ctx_rows, model), F32)],
        flops=8 * ctx_rows * model * feed,
        name="feed_weights",
    )
    h2_own, dg, du, dd = lax.optimization_barrier((h2_parts[0], dg, du, dd))
    dg, du, dd = lax.psum((dg, du, dd), ("dp", "ctx"))

    resid_grad, low_share, gain2_part = call(
        resid_back_kernel,
        [resid, og, gain2, h2_own] + h2_got,
        [out((share, model), F32), out((share, model), BF), out((1, model), F32)],
        name="resid_back",
    )
    low_parts = [low_share] + swaps([low_share] * mp, "mp")

    o_mine, o_other = call(
        o_weights_kernel,
        [here_dp[None], att_t] + low_parts,
        [out((q_width // 2, model), BF)] * 2,
        in_specs={0: SMEM},
        scratch=[pltpu.VMEM((ctx_rows, model), BF)],
        name="o_weights",
    )
    bit = ((here_ctx & 1) ^ ((here_ctx >> 1) & 1))[None]
    o_chunks = sum_over_ctx(o_mine, o_other, bit, few)
    first_low, _ = lax.optimization_barrier((low_parts[0], o_other))
    low_parts = [first_low] + low_parts[1:]
    head_rows = pl.BlockSpec((seq_rows, width), lambda h: (0, h), **buffers)
    ql, dk, dv, gq_part = call(
        lambda *refs: attend_back_kernel(joined, ctx_rows, width, mp, *refs),
        [block_order, last_block, kpos, qpos, qlow]
        + low_parts
        + [o_weight, qt, qlin, ot, sums, gq_col, cosines_t, sines_t]
        + keys
        + values,
        [
            out((q_width, ctx_rows), BF),
            out((seq_rows, k_width), F32),
            out((seq_rows, k_width), F32),
            out((width, 1), F32),
        ],
        grid=(kv_heads,),
        in_specs={
            0: SMEM,
            1: SMEM,
            5 + mp: wo_block,
            6 + mp: t_block,
            7 + mp: t_block,
            8 + mp: t_block,
            9 + mp: sums_block,
            **{13 + mp + m * n + i: by_head[i] for m in range(2) for i in range(n)},
        },
        out_specs={0: t_block, 1: head_rows, 2: head_rows},
        scratch=copies
        + [
            pltpu.VMEM((width, lanes), F32),
            pltpu.VMEM((ctx_rows, model), BF),
            pltpu.VMEM((group_width, ctx_rows), F32),
        ],
        flops=5 * pair_flops,
        name="attend_back",
    )

    f_got = swaps(f_parts, "mp")
    dk, *f_got = lax.optimization_barrier((dk, *f_got))
    output = call(
        sum_kernel, [resid, f_parts[0]] + f_got, [out((share, model), BF)], name="output"
    )[0][None]

    m = len(groups)
    starts = [sum(len(slots) for slots in groups[:i]) for i in range(m)]
    slot_at = [slot for slots in groups for slot in slots]

    def stepped(i, rows, columns):
        first, size = starts[i], len(groups[i])
        return pl.BlockSpec((rows, columns), lambda s: (jnp.clip(s - first, 0, size - 1), 0))

    def ordered(rows, columns):
        def place(s):
            slot = s
            for step, value in enumerate(slot_at):
                if step != value:
                    slot = jnp.where(s == step, value, slot)
            return slot, 0

        return pl.BlockSpec((rows, columns), place)

    kl, vl, mine, other, gain1_part, gk_part = call(
        lambda *refs: weights_kernel(groups, *refs),
        [here_dp[None], ql, dk, dv, cosines, sines, gk_row]
        + hiddens
        + klins
        + [q_weight, key_matrix, value_matrix, norm1_gain.astype(F32)[:, None]],
        [out((seq_rows, k_width), BF)] * 2
        + [out((model // 2, q_width + 2 * k_width), BF)] * 2
        + [out((model, 1), F32), out((1, width), F32)],
        grid=(ctx,),
        in_specs={
            0: SMEM,
            2: ordered(ctx_rows, k_width),
            3: ordered(ctx_rows, k_width),
            4: ordered(ctx_rows, width),
            5: ordered(ctx_rows, width),
            **{7 + i: stepped(i, ctx_rows, model) for i in range(m)},
            **{7 + m + i: stepped(i, ctx_rows, k_width) for i in range(m)},
        },
        out_specs={0: ordered(ctx_rows, k_width), 1: ordered(ctx_rows, k_width)},
        scratch=[pltpu.VMEM((model, q_width + 2 * k_width), F32)],
        name="weights",
    )

    def hidden_back(slots):
        size = len(slots)
        own = slots == (0,)
        ins = ([ql, q_weight] if own else []) + [kl, vl, key_matrix, value_matrix]
        skip = 2 if own else 0
        block = slot_blocks(slots, ctx_rows, k_width)
        parts = call(
            lambda *refs: hidden_back_kernel(own, mp, *refs),
            ins,
            [out((size, share, model), F32)] + [out((size, share, model), BF)] * (mp - 1),
            grid=(size,),
            in_specs={skip: block, skip + 1: block},
            out_specs={
                j: pl.BlockSpec((1, share, model), lambda i: (i, 0, 0)) for j in range(mp)
            },
            name="hidden_back",
        )
        return parts, swaps(parts, "mp")

    terms = []
    if few:
        for slots in ((2,), (1, 3)):
            parts, got = hidden_back(slots)
            for i, slot in enumerate(slots):
                summed = sum_parts([p[i] for p in [parts[0]] + got], BF)
                terms.append(to_ctx(summed, slot))
    else:
        parts, got = hidden_back(tuple(range(1, ctx)))
        summed = (parts[0] + sum(p.astype(F32) for p in got)).astype(BF)
        padded = jnp.concatenate([jnp.zeros_like(summed[:1]), summed], axis=0)
        padded = jnp.concatenate([padded, padded], axis=0)
        natural = lax.dynamic_slice_in_dim(padded, (ctx - here_ctx) % ctx, ctx, 0)
        terms.append(lax.psum_scatter(natural, "ctx", scatter_dimension=0, tiled=False))
    parts, got = hidden_back((0,))
    chunks = sum_over_ctx(mine, other, bit, few, (dg, du, dd, got[-1]))
    terms = [p[0] for p in [parts[0]] + got] + terms
    input_grad = call(
        input_back_kernel, [tok, resid_grad, gain1] + terms, [out((share, model), F32)], name="input_back"
    )[0][None]

    if few:
        spots = jnp.concatenate([bit, 1 - bit]) + 2 * here_dp
        spots = jnp.concatenate([spots, jnp.concatenate([bit, 1 - bit]) + 2 * (1 - here_dp)])
    else:
        spots = jnp.stack([here_dp, 1 - here_dp])
    q_w_grad, k_w_grad, v_w_grad, o_w_grad = call(
        lambda *refs: spread_kernel(q_width, k_width, len(chunks), *refs),
        [spots] + chunks + o_chunks,
        [
            out((model, q_width), F32),
            out((model, k_width), F32),
            out((model, k_width), F32),
            out((q_width, model), F32),
        ],
        in_specs={0: SMEM},
        name="spread",
    )

    gains = jnp.concatenate(
        [gain1_part.reshape(-1), gain2_part.reshape(-1), gq_part.reshape(-1), gk_part.reshape(-1)]
    )
    if few:
        for axis in ("dp", "mp", "ctx"):
            for step in (1, 2, 4):
                if step < lax.axis_size(axis):
                    gains = gains + swap(gains, axis, step)
    else:
        gains = lax.psum(gains, ("dp", "ctx", "mp"))
    return (
        output,
        input_grad,
        gains[:model],
        q_w_grad,
        k_w_grad,
        v_w_grad,
        gains[2 * model : 2 * model + width],
        gains[2 * model + width :],
        o_w_grad,
        gains[model : 2 * model],
        dg.astype(F32),
        du.astype(F32),
        dd.astype(F32),
    )


def solution(mesh):
    placed = (
        P("dp", ("ctx", "mp"), None),
        P(),
        P(None, "mp"),
        P(None, "mp"),
        P(None, "mp"),
        P(),
        P(),
        P("mp", None),
        P(),
        P(None, "mp"),
        P(None, "mp"),
        P("mp", None),
        P("dp", ("ctx", "mp"), None),
        P("dp", None),
        P(),
    )
    return jax.shard_map(
        on_device,
        mesh=mesh,
        in_specs=placed,
        out_specs=(
            P("dp", ("ctx", "mp"), None),
            P("dp", ("ctx", "mp"), None),
            P(),
            P(None, "mp"),
            P(None, "mp"),
            P(None, "mp"),
            P(),
            P(),
            P("mp", None),
            P(),
            P(None, "mp"),
            P(None, "mp"),
            P("mp", None),
        ),
        check_vma=False,
    )
```

```python
import math

import jax
import jax.numpy as jnp
from jax import lax
from jax.experimental import pallas as pl
from jax.experimental.pallas import tpu as pltpu
from jax.sharding import PartitionSpec as P

EPS = 1e-06
THETA = 1000000.0
LOG2E = 1.4426950408889634
BF = jnp.bfloat16
F32 = jnp.float32
VMEM_LIMIT = 52 * 1024 * 1024


def dot(left, right, left_dim, right_dim):
    return lax.dot_general(
        left, right, (((left_dim,), (right_dim,)), ((), ())), preferred_element_type=F32
    )


def whole_spec(array):
    rank = len(array.shape)
    return pl.BlockSpec(array.shape, lambda *_: (0,) * rank)


SMEM = pl.BlockSpec(memory_space=pltpu.SMEM)


def call(kernel, ins, outs, grid=(1,), in_specs=None, out_specs=None, scratch=(), flops=0, name=None):
    in_specs = in_specs or {}
    out_specs = out_specs or {}
    return pl.pallas_call(
        kernel,
        grid=grid,
        in_specs=[in_specs.get(i, whole_spec(a)) for i, a in enumerate(ins)],
        out_specs=[out_specs.get(i, whole_spec(a)) for i, a in enumerate(outs)],
        out_shape=list(outs),
        scratch_shapes=list(scratch),
        compiler_params=pltpu.CompilerParams(vmem_limit_bytes=VMEM_LIMIT),
        cost_estimate=pl.CostEstimate(flops=0, bytes_accessed=0, transcendentals=0),
        name=name,
    )(*ins)


def out(shape, dtype):
    return jax.ShapeDtypeStruct(shape, dtype)


def swap(value, axis, step):
    size = lax.axis_size(axis)
    return lax.ppermute(value, axis, [(i, i ^ step) for i in range(size)])


def swaps(values, axis):
    order = sorted(range(1, len(values)), key=lambda j: -bin(j).count("1"))
    got = {j: swap(values[j], axis, j) for j in order}
    return [got[j] for j in range(1, len(values))]


def from_ctx(value, step):
    size = lax.axis_size("ctx")
    return lax.ppermute(value, "ctx", [((i + step) % size, i) for i in range(size)])


def to_ctx(value, step):
    size = lax.axis_size("ctx")
    return lax.ppermute(value, "ctx", [(i, (i + step) % size) for i in range(size)])


def norm_kernel(rows_ref, gain_ref, normed_ref):
    rows = rows_ref[...].astype(F32)
    factor = lax.rsqrt(jnp.mean(rows * rows, axis=-1, keepdims=True) + EPS)
    normed_ref[...] = (rows * factor * gain_ref[...]).astype(BF)


def resid_kernel(tok_ref, own_ref, *refs):
    *parts, gain_ref, resid_ref, normed_ref = refs
    rows = tok_ref[...].astype(F32) + own_ref[...]
    for part in parts:
        rows = rows + part[...].astype(F32)
    resid_ref[...] = rows
    factor = lax.rsqrt(jnp.mean(rows * rows, axis=-1, keepdims=True) + EPS)
    normed_ref[...] = (rows * factor * gain_ref[...]).astype(BF)


def norm_back(rows, gain, gradient):
    factor = lax.rsqrt(jnp.mean(rows * rows, axis=-1, keepdims=True) + EPS)
    scaled = gradient * gain
    inner = jnp.mean(scaled * rows, axis=-1, keepdims=True)
    return factor * scaled - rows * (factor * factor * factor) * inner, gradient * rows * factor


def resid_back_kernel(resid_ref, grad_ref, gain_ref, own_ref, *refs):
    *parts, full_ref, low_ref, gain_grad_ref = refs
    gradient = own_ref[...]
    for part in parts:
        gradient = gradient + part[...].astype(F32)
    back, terms = norm_back(resid_ref[...], gain_ref[...], gradient)
    total = grad_ref[...].astype(F32) + back
    full_ref[...] = total
    low_ref[...] = total.astype(BF)
    gain_grad_ref[...] = jnp.sum(terms, axis=0, keepdims=True)


def input_back_kernel(tok_ref, resid_grad_ref, gain_ref, *refs):
    *parts, result_ref = refs
    gradient = parts[0][...].astype(F32)
    for part in parts[1:]:
        gradient = gradient + part[...].astype(F32)
    back, _ = norm_back(tok_ref[...].astype(F32), gain_ref[...], gradient)
    result_ref[...] = resid_grad_ref[...] + back


def sum_kernel(*refs):
    *parts, result_ref = refs
    total = parts[0][...].astype(F32)
    for part in parts[1:]:
        total = total + part[...].astype(F32)
    result_ref[...] = total.astype(result_ref.dtype)


def sum_parts(parts, dtype):
    return call(sum_kernel, parts, [out(parts[0].shape, dtype)], name="sum_parts")[0]


def key_rows(linear, gain, cosines, sines):
    heads = []
    for start in range(0, linear.shape[1], gain.shape[1]):
        rows = linear[:, start : start + gain.shape[1]]
        factor = lax.rsqrt(jnp.mean(rows * rows, axis=-1, keepdims=True) + EPS)
        normed = rows * factor * gain
        turned = pltpu.roll(normed, normed.shape[1] // 2, 1)
        heads.append((normed * cosines + turned * sines).astype(BF))
    return heads


def key_value_part(hidden, wk_ref, wv_ref, gk_ref, cos_ref, sin_ref, k_ref, v_ref, klin_ref):
    linear = dot(hidden, wk_ref[...], 1, 0)
    klin_ref[...] = linear
    width = gk_ref.shape[1]
    for head, rows in enumerate(key_rows(linear, gk_ref[...], cos_ref[...], sin_ref[...])):
        k_ref[:, head * width : (head + 1) * width] = rows
    v_ref[...] = dot(hidden, wv_ref[...], 1, 0).astype(BF)


def turn_rows(value):
    half = value.shape[0] // 2
    return jnp.concatenate([-value[half:], value[:half]], axis=0)


def own_kernel(count, *refs):
    parts = refs[:count]
    (wq_ref, wk_ref, wv_ref, gq_ref, gk_ref, cos_t_ref, sin_t_ref, cos_ref, sin_ref) = refs[
        count : count + 9
    ]
    qt_ref, qlin_ref, k_ref, v_ref, klin_ref, hidden_ref = refs[count + 9 :]
    share = parts[0].shape[0]
    for j, part in enumerate(parts):
        hidden_ref[j * share : (j + 1) * share, :] = part[...]
    hidden = hidden_ref[...]
    key_value_part(hidden, wk_ref, wv_ref, gk_ref, cos_ref, sin_ref, k_ref, v_ref, klin_ref)
    linear = dot(wq_ref[...], hidden, 0, 1)
    qlin_ref[...] = linear
    width = gq_ref.shape[0]
    for start in range(0, linear.shape[0], width):
        rows = linear[start : start + width]
        factor = lax.rsqrt(jnp.mean(rows * rows, axis=0, keepdims=True) + EPS)
        normed = rows * factor * gq_ref[...]
        qt_ref[start : start + width, :] = (
            normed * cos_t_ref[...] + turn_rows(normed) * sin_t_ref[...]
        ).astype(BF)


def remote_kernel(count, *refs):
    parts = refs[:count]
    wk_ref, wv_ref, gk_ref, cos_ref, sin_ref = refs[count : count + 5]
    k_ref, v_ref, klin_ref, hidden_ref = refs[count + 5 :]
    share = parts[0].shape[1]
    for j, part in enumerate(parts):
        hidden_ref[j * share : (j + 1) * share, :] = part[0]
    key_value_part(
        hidden_ref[...], wk_ref, wv_ref, gk_ref, cos_ref, sin_ref, k_ref, v_ref, klin_ref
    )


def place_slots(target_ref, refs, groups, rows):
    if len(refs) == 1:
        return refs[0]
    for ref, group in zip(refs, groups):
        for i, slot in enumerate(group):
            target_ref[pl.ds(slot * rows, rows), :] = ref[i * rows : (i + 1) * rows, :]
    return target_ref


def lanes_of(ref, half_index, half, width):
    heads = [
        ref[start : start + width, half_index * half : (half_index + 1) * half]
        for start in range(0, ref.shape[0], width)
    ]
    return jnp.concatenate(heads, axis=1)


def attend_kernel(groups, ctx_rows, width, mp, *refs):
    n = len(groups)
    order_ref, last_ref, kpos_ref, qpos_ref, qlow_ref, qt_ref, wo_ref = refs[:7]
    k_refs, v_refs = refs[7 : 7 + n], refs[7 + n : 7 + 2 * n]
    rest = refs[7 + 2 * n :]
    ot_ref, attt_ref, sums_ref = rest[:3]
    part_refs = rest[3 : 3 + mp]
    k_all, v_all, numer, sums, projected = rest[3 + mp :]
    half = ctx_rows // 2
    share = ctx_rows // mp
    per_group = qt_ref.shape[0] // width
    k_all = place_slots(k_all, k_refs, groups, ctx_rows)
    v_all = place_slots(v_all, v_refs, groups, ctx_rows)
    scale = LOG2E / math.sqrt(width)
    for t in range(2):
        queries = lanes_of(qt_ref, t, half, width)
        qpos = jnp.concatenate([qpos_ref[:, t * half : (t + 1) * half]] * per_group, axis=1)
        qlow = jnp.concatenate([qlow_ref[:, t * half : (t + 1) * half]] * per_group, axis=1)
        numer[...] = jnp.zeros_like(numer)
        sums[...] = jnp.zeros_like(sums)

        def block(i):
            start = pl.multiple_of(order_ref[i] * half, half)
            scores = dot(k_all[pl.ds(start, half), :], queries, 1, 0)
            kpos = kpos_ref[...] + i * half
            seen = (kpos <= qpos) & (kpos >= qlow)
            weights = jnp.where(seen, jnp.exp2(scores * scale), 0.0)
            added = dot(v_all[pl.ds(start, half), :], weights.astype(BF), 0, 0)
            return jnp.sum(weights, axis=0, keepdims=True), added

        def step(i, carry):
            first_sum, first = block(2 * i)
            second_sum, second = block(2 * i + 1)
            sums[...] += first_sum + second_sum
            numer[...] += first + second
            return carry

        lax.fori_loop(0, last_ref[t] // 2 + 1, step, 0)
        total = sums[...]
        sums_ref[0, t : t + 1, :] = total
        result = numer[...] / total
        for head in range(per_group):
            piece = result[:, head * half : (head + 1) * half]
            ot_ref[head * width : (head + 1) * width, t * half : (t + 1) * half] = piece
            attt_ref[head * width : (head + 1) * width, t * half : (t + 1) * half] = piece.astype(BF)
    added = dot(attt_ref[...], wo_ref[...], 0, 0)
    group = pl.program_id(0)

    @pl.when(group == 0)
    def _():
        projected[...] = added

    @pl.when(group > 0)
    def _():
        projected[...] += added

    @pl.when(group == pl.num_programs(0) - 1)
    def _():
        for j, ref in enumerate(part_refs):
            ref[...] = projected[j * share : (j + 1) * share, :].astype(ref.dtype)


def feed_kernel(count, *refs):
    peer_ref = refs[0]
    parts = refs[1 : 1 + count]
    grad_ref, wg_ref, wu_ref, wd_ref = refs[1 + count : 5 + count]
    hidden_ref, grads_ref, act_ref, gg_ref, ug_ref = refs[5 + count : 10 + count]
    part_refs = refs[10 + count : 10 + 2 * count]
    total = refs[10 + 2 * count]
    share = parts[0].shape[0]
    step = pl.program_id(0)

    @pl.when(step == 0)
    def _():
        for j, part in enumerate(parts):
            hidden_ref[j * share : (j + 1) * share, :] = part[...]
            place = pl.multiple_of(peer_ref[j] * share, share)
            grads_ref[j * share : (j + 1) * share, :] = grad_ref[pl.ds(place, share), :]

    hidden = hidden_ref[...]
    tile = wg_ref.shape[1]
    both = jnp.concatenate([wg_ref[...], wu_ref[...]], axis=1)
    product = dot(hidden, both, 1, 0)
    gate, up = product[:, :tile], product[:, tile:]
    act_grad = dot(grads_ref[...], wd_ref[...], 1, 1)
    sig = 0.5 * jnp.tanh(0.5 * gate) + 0.5
    silu = gate * sig
    act_ref[...] = (silu * up).astype(BF)
    gate_grad = (act_grad * up * sig * (1.0 + gate * (1.0 - sig))).astype(BF)
    up_grad = (act_grad * silu).astype(BF)
    gg_ref[...] = gate_grad
    ug_ref[...] = up_grad
    added = dot(jnp.concatenate([gate_grad, up_grad], axis=1), both, 1, 1)

    @pl.when(step == 0)
    def _():
        total[...] = added

    @pl.when(step > 0)
    def _():
        total[...] += added

    @pl.when(step == pl.num_programs(0) - 1)
    def _():
        for j, ref in enumerate(part_refs):
            ref[...] = total[j * share : (j + 1) * share, :].astype(ref.dtype)


def feed_weights_kernel(hidden_ref, grads_ref, act_ref, gg_ref, ug_ref, wd_ref, *refs):
    dg_ref, du_ref, dd_ref = refs[:3]
    *part_refs, total = refs[3:]
    share = part_refs[0].shape[0]
    step = pl.program_id(0)
    dg_ref[...] = dot(hidden_ref[...], gg_ref[...], 0, 0).astype(BF)
    du_ref[...] = dot(hidden_ref[...], ug_ref[...], 0, 0).astype(BF)
    dd_ref[...] = dot(act_ref[...], grads_ref[...], 0, 0).astype(BF)
    added = dot(act_ref[...], wd_ref[...], 1, 0)

    @pl.when(step == 0)
    def _():
        total[...] = added

    @pl.when(step > 0)
    def _():
        total[...] += added

    @pl.when(step == pl.num_programs(0) - 1)
    def _():
        for j, ref in enumerate(part_refs):
            ref[...] = total[j * share : (j + 1) * share, :].astype(ref.dtype)


def attend_back_kernel(groups, ctx_rows, width, mp, *refs):
    n = len(groups)
    order_ref, last_ref, kpos_ref, qpos_ref, qlow_ref = refs[:5]
    low_refs = refs[5 : 5 + mp]
    wo_ref, qt_ref, qlin_ref, ot_ref, sums_ref, gq_ref, cos_t_ref, sin_t_ref = refs[
        5 + mp : 13 + mp
    ]
    at = 13 + mp
    k_refs, v_refs = refs[at : at + n], refs[at + n : at + 2 * n]
    at += 2 * n
    ql_ref, dk, dv, gqg_ref = refs[at : at + 4]
    k_all, v_all, dq, low_all, dqt = refs[at + 4 :]
    half = ctx_rows // 2
    share = ctx_rows // mp
    per_group = qt_ref.shape[0] // width
    scale = LOG2E / math.sqrt(width)
    score_scale = 1.0 / math.sqrt(width)
    group = pl.program_id(0)
    k_all = place_slots(k_all, k_refs, groups, ctx_rows)
    v_all = place_slots(v_all, v_refs, groups, ctx_rows)
    dk[...] = jnp.zeros_like(dk)
    dv[...] = jnp.zeros_like(dv)

    @pl.when(group == 0)
    def _():
        for j, ref in enumerate(low_refs):
            low_all[j * share : (j + 1) * share, :] = ref[...]
        gqg_ref[...] = jnp.zeros_like(gqg_ref)

    att_grad = dot(wo_ref[...], low_all[...], 1, 1).astype(BF).astype(F32)
    for t in range(2):
        queries = lanes_of(qt_ref, t, half, width)
        pre = lanes_of(ot_ref, t, half, width)
        grads = jnp.concatenate(
            [
                att_grad[h * width : (h + 1) * width, t * half : (t + 1) * half]
                for h in range(per_group)
            ],
            axis=1,
        )
        inverse = 1.0 / sums_ref[0, t : t + 1, :]
        scaled = (grads * inverse).astype(BF)
        shift = jnp.sum(grads * pre, axis=0, keepdims=True) * inverse
        qpos = jnp.concatenate([qpos_ref[:, t * half : (t + 1) * half]] * per_group, axis=1)
        qlow = jnp.concatenate([qlow_ref[:, t * half : (t + 1) * half]] * per_group, axis=1)
        dq[...] = jnp.zeros_like(dq)

        def block(i):
            start = pl.multiple_of(order_ref[i] * half, half)
            keys = k_all[pl.ds(start, half), :]
            scores = dot(keys, queries, 1, 0)
            prob_grad = dot(v_all[pl.ds(start, half), :], scaled, 1, 0)
            kpos = kpos_ref[...] + i * half
            seen = (kpos <= qpos) & (kpos >= qlow)
            weights = jnp.where(seen, jnp.exp2(scores * scale), 0.0)
            score_grad = (weights * (prob_grad - shift)).astype(BF)
            dv[pl.ds(start, half), :] += dot(weights.astype(BF), scaled, 1, 1)
            dk[pl.ds(start, half), :] += dot(score_grad, queries, 1, 1)
            return dot(keys, score_grad, 0, 0)

        def step(i, carry):
            first = block(2 * i)
            dq[...] += first + block(2 * i + 1)
            return carry

        lax.fori_loop(0, last_ref[t] // 2 + 1, step, 0)
        for head in range(per_group):
            dqt[head * width : (head + 1) * width, t * half : (t + 1) * half] = dq[
                :, head * half : (head + 1) * half
            ]
    for head in range(per_group):
        rows = qlin_ref[head * width : (head + 1) * width, :]
        rotated = dqt[head * width : (head + 1) * width, :] * score_scale
        gradient = rotated * cos_t_ref[...] - turn_rows(rotated) * sin_t_ref[...]
        factor = lax.rsqrt(jnp.mean(rows * rows, axis=0, keepdims=True) + EPS)
        gained = gradient * gq_ref[...]
        inner = jnp.mean(gained * rows, axis=0, keepdims=True)
        ql_ref[head * width : (head + 1) * width, :] = (
            factor * gained - rows * (factor * factor * factor) * inner
        ).astype(BF)
        gqg_ref[...] += jnp.sum(gradient * rows * factor, axis=1, keepdims=True)


def hidden_back_kernel(own, mp, *refs):
    if own:
        ql_ref, wq_ref, *refs = refs
    kl_ref, vl_ref, wk_ref, wv_ref = refs[:4]
    part_refs = refs[4:]
    share = part_refs[0].shape[1]
    total = dot(kl_ref[...], wk_ref[...], 1, 1) + dot(vl_ref[...], wv_ref[...], 1, 1)
    if own:
        total = total + dot(ql_ref[...], wq_ref[...], 0, 1)
    for j, ref in enumerate(part_refs):
        ref[0] = total[j * share : (j + 1) * share, :].astype(ref.dtype)


def o_weights_kernel(core_ref, attt_ref, *refs):
    *low_refs, mine_ref, other_ref, low_all = refs
    share = low_refs[0].shape[0]
    for j, ref in enumerate(low_refs):
        low_all[j * share : (j + 1) * share, :] = ref[...]
    rows = mine_ref.shape[0]
    core = core_ref[0]
    for ref, at in ((mine_ref, core), (other_ref, 1 - core)):
        here = pl.ds(pl.multiple_of(at * rows, rows), rows)
        ref[...] = dot(attt_ref[here, :], low_all[...], 1, 0).astype(BF)


def weights_kernel(groups, *refs):
    n = len(groups)
    core_ref, ql_ref, dk_ref, dv_ref, cos_ref, sin_ref, gk_ref = refs[:7]
    hidden_refs, klin_refs = refs[7 : 7 + n], refs[7 + n : 7 + 2 * n]
    (
        wq_ref, wk_ref, wv_ref, gain_ref, kl_ref, vl_ref,
        mine_ref, other_ref, gain_grad_ref, gkg_ref, accum,
    ) = refs[7 + 2 * n :]
    step = pl.program_id(0)
    model = gain_ref.shape[0]
    q_width, k_width = ql_ref.shape[0], dk_ref.shape[1]
    width = gk_ref.shape[1]
    score_scale = 1.0 / math.sqrt(width)

    @pl.when(step == 0)
    def _():
        accum[:, :q_width] = dot(hidden_refs[0][...], ql_ref[...], 0, 1)
        accum[:, q_width:] = jnp.zeros_like(accum[:, q_width:])
        gkg_ref[...] = jnp.zeros_like(gkg_ref)

    first = 0
    for hidden_ref, klin_ref, slots in zip(hidden_refs, klin_refs, groups):

        @pl.when((step >= first) & (step < first + len(slots)))
        def _():
            for start in range(0, k_width, width):
                head = slice(start, start + width)
                rotated = dk_ref[:, head] * score_scale
                gradient = rotated * cos_ref[...] - pltpu.roll(rotated, width // 2, 1) * sin_ref[...]
                back, terms = norm_back(klin_ref[:, head], gk_ref[...], gradient)
                kl_ref[:, head] = back.astype(BF)
                gkg_ref[...] += jnp.sum(terms, axis=0, keepdims=True)
            vl_ref[...] = dv_ref[...].astype(BF)
            hidden = hidden_ref[...]
            accum[:, q_width : q_width + k_width] += dot(hidden, kl_ref[...], 0, 0)
            accum[:, q_width + k_width :] += dot(hidden, vl_ref[...], 0, 0)

        first += len(slots)

    @pl.when(step == pl.num_programs(0) - 1)
    def _():
        terms = jnp.sum(accum[:, :q_width] * wq_ref[...].astype(F32), axis=1, keepdims=True)
        terms += jnp.sum(
            accum[:, q_width : q_width + k_width] * wk_ref[...].astype(F32), axis=1, keepdims=True
        )
        terms += jnp.sum(
            accum[:, q_width + k_width :] * wv_ref[...].astype(F32), axis=1, keepdims=True
        )
        gain_grad_ref[...] = terms / gain_ref[...]
        rows = mine_ref.shape[0]
        core = core_ref[0]
        mine_ref[...] = accum[pl.ds(pl.multiple_of(core * rows, rows), rows), :].astype(BF)
        other_ref[...] = accum[pl.ds(pl.multiple_of((1 - core) * rows, rows), rows), :].astype(BF)


def split_kernel(place_ref, mine_ref, got_ref, keep_ref, send_ref):
    rows = keep_ref.shape[0]
    for ref, at in ((keep_ref, place_ref[0]), (send_ref, 1 - place_ref[0])):
        here = pl.ds(pl.multiple_of(at * rows, rows), rows)
        ref[...] = (mine_ref[here, :].astype(F32) + got_ref[here, :].astype(F32)).astype(ref.dtype)


def spread_kernel(q_width, k_width, count, *refs):
    place_ref = refs[0]
    chunks, o_chunks = refs[1 : 1 + count], refs[1 + count : 1 + 2 * count]
    dq_ref, dk_ref, dv_ref, do_ref = refs[1 + 2 * count :]
    for i, ref in enumerate(chunks):
        rows = ref.shape[0]
        here = pl.ds(pl.multiple_of(place_ref[i] * rows, rows), rows)
        dq_ref[here, :] = ref[:, :q_width].astype(F32)
        dk_ref[here, :] = ref[:, q_width : q_width + k_width].astype(F32)
        dv_ref[here, :] = ref[:, q_width + k_width :].astype(F32)
    for i, ref in enumerate(o_chunks):
        rows = ref.shape[0]
        here = pl.ds(pl.multiple_of(place_ref[i] * rows, rows), rows)
        do_ref[here, :] = ref[...].astype(F32)


def sum_over_ctx(mine, other, part, few, after=()):
    got = swap(other, "dp", 1)
    if not few:
        chunk = lax.psum(sum_parts([mine, got], BF), "ctx")
        return [chunk, swap(chunk, "dp", 1)]
    rows = mine.shape[0] // 2
    keep, send = call(
        split_kernel,
        [part, mine, got],
        [out((rows, mine.shape[1]), F32), out((rows, mine.shape[1]), BF)],
        in_specs={0: SMEM},
        name="split",
    )
    pair = sum_parts([keep, swap(send, "ctx", 1)], BF)
    if after:
        pair, *_ = lax.optimization_barrier((pair, *after))
    total = sum_parts([pair, swap(pair, "ctx", 3)], BF)
    chunks = [total, swap(total, "ctx", 1)]
    return chunks + [swap(c, "dp", 1) for c in chunks]


def slot_blocks(group, rows, width):
    first = group[0]
    gap = group[1] - group[0] if len(group) > 1 else 1
    return pl.BlockSpec((rows, width), lambda i: (first + gap * i, 0))


def on_device(
    tokens,
    norm1_gain,
    q_weight,
    key_matrix,
    value_matrix,
    q_gain,
    k_gain,
    o_weight,
    norm2_gain,
    gate_weight,
    up_weight,
    down_weight,
    out_grad,
    lengths,
    pairing,
):
    width = q_gain.shape[0]
    model = tokens.shape[2]
    share = tokens.shape[1]
    mp = lax.axis_size("mp")
    ctx = lax.axis_size("ctx")
    q_width = q_weight.shape[1]
    k_width = key_matrix.shape[1]
    kv_heads = k_width // width
    group_width = q_width // kv_heads
    feed = gate_weight.shape[1]
    ctx_rows = share * mp
    half = ctx_rows // 2
    seq_rows = ctx_rows * ctx
    few = ctx == 4
    here_ctx = lax.axis_index("ctx")
    here_mp = lax.axis_index("mp")
    here_dp = lax.axis_index("dp")
    gain1 = norm1_gain.astype(F32)[None, :]
    gain2 = norm2_gain.astype(F32)[None, :]
    gq_col = q_gain.astype(F32)[:, None]
    gk_row = k_gain.astype(F32)[None, :]
    tok = tokens[0]
    og = out_grad[0]

    h1_share = call(norm_kernel, [tok, gain1], [out((share, model), BF)], name="norm1")[0]
    own_parts = [h1_share] + swaps([h1_share] * mp, "mp")
    if few:
        near = {k: from_ctx(h1_share, k) for k in (1, 3)}
        own_parts[0], near[1], near[3] = lax.optimization_barrier((own_parts[0], near[1], near[3]))

    slot_ctx = (here_ctx + jnp.arange(ctx, dtype=jnp.int32)) % ctx
    slot_pair = jnp.sum(
        jnp.where(slot_ctx[:, None] == jnp.arange(ctx, dtype=jnp.int32)[None, :], pairing[None, :], 0),
        axis=1,
    )
    peers = here_mp ^ jnp.arange(mp, dtype=jnp.int32)
    rows_in = (peers[:, None] * share + jnp.arange(share, dtype=jnp.int32)[None, :]).reshape(-1)
    blocks = jnp.where(
        rows_in[None, :] < half, slot_pair[:, None], 2 * ctx - 1 - slot_pair[:, None]
    )
    positions = (blocks * half + (rows_in % half)[None, :]).reshape(-1)
    block_ids = blocks[:, ::half].reshape(-1)
    block_order = jnp.sum(
        jnp.where(
            block_ids[None, :] == jnp.arange(2 * ctx, dtype=jnp.int32)[:, None],
            jnp.arange(2 * ctx, dtype=jnp.int32)[None, :],
            0,
        ),
        axis=1,
    )
    last_block = block_ids[:2]
    own_pos = positions[:ctx_rows]
    doc_ends = jnp.cumsum(lengths[0])
    own_low = jnp.max(
        jnp.where(doc_ends[None, :] <= own_pos[:, None], doc_ends[None, :], 0), axis=1
    )
    qpos, qlow, kpos = own_pos[None, :], own_low[None, :], (rows_in % half)[:half, None]
    frequency = THETA ** (-(jnp.arange(width // 2, dtype=F32) * 2.0) / width)
    angles = positions.astype(F32)[:, None] * frequency[None, :]
    cos_half, sin_half = jnp.cos(angles), jnp.sin(angles)
    cosines = jnp.concatenate([cos_half, cos_half], axis=1)
    sines = jnp.concatenate([-sin_half, sin_half], axis=1)
    angles_t = frequency[:, None] * own_pos.astype(F32)[None, :]
    cos_t, sin_t = jnp.cos(angles_t), jnp.sin(angles_t)
    cosines_t = jnp.concatenate([cos_t, cos_t], axis=0)
    sines_t = jnp.concatenate([sin_t, sin_t], axis=0)

    qt, qlin, k_own, v_own, klin_own, h1_own = call(
        lambda *refs: own_kernel(mp, *refs),
        own_parts
        + [q_weight, key_matrix, value_matrix, gq_col, gk_row, cosines_t, sines_t, cosines, sines],
        [
            out((q_width, ctx_rows), BF),
            out((q_width, ctx_rows), F32),
            out((ctx_rows, k_width), BF),
            out((ctx_rows, k_width), BF),
            out((ctx_rows, k_width), F32),
            out((ctx_rows, model), BF),
        ],
        in_specs={
            mp + 7: pl.BlockSpec((ctx_rows, width), lambda i: (0, 0)),
            mp + 8: pl.BlockSpec((ctx_rows, width), lambda i: (0, 0)),
        },
        flops=2 * ctx_rows * model * (q_width + 2 * k_width),
        name="own_rows",
    )
    if few:
        late_share, _ = lax.optimization_barrier((h1_share, k_own))
        far = from_ctx(late_share, 2)
        remote = [((1, 3), jnp.stack([near[1], near[3]])), ((2,), far[None])]
    else:
        every = lax.all_gather(h1_share, "ctx", axis=0)
        every = jnp.concatenate([every, every], axis=0)
        every = lax.dynamic_slice_in_dim(every, here_ctx + 1, ctx - 1, 0)
        remote = [(tuple(range(1, ctx)), every)]
    remote_parts = [[value] + swaps([value] * mp, "mp") for _, value in remote]
    groups = [(0,)] + [slots for slots, _ in remote]
    keys, values, klins, hiddens = [k_own], [v_own], [klin_own], [h1_own]
    for (slots, _), parts in zip(remote, remote_parts):
        size = len(slots)
        k_new, v_new, klin_new, h1_new = call(
            lambda *refs: remote_kernel(mp, *refs),
            parts + [key_matrix, value_matrix, gk_row, cosines, sines],
            [
                out((size * ctx_rows, k_width), BF),
                out((size * ctx_rows, k_width), BF),
                out((size * ctx_rows, k_width), F32),
                out((size * ctx_rows, model), BF),
            ],
            grid=(size,),
            in_specs={
                **{j: pl.BlockSpec((1, share, model), lambda i: (i, 0, 0)) for j in range(mp)},
                mp + 3: slot_blocks(slots, ctx_rows, width),
                mp + 4: slot_blocks(slots, ctx_rows, width),
            },
            out_specs={
                0: pl.BlockSpec((ctx_rows, k_width), lambda i: (i, 0)),
                1: pl.BlockSpec((ctx_rows, k_width), lambda i: (i, 0)),
                2: pl.BlockSpec((ctx_rows, k_width), lambda i: (i, 0)),
                3: pl.BlockSpec((ctx_rows, model), lambda i: (i, 0)),
            },
            flops=4 * size * ctx_rows * model * k_width,
            name="remote_rows",
        )
        keys.append(k_new)
        values.append(v_new)
        klins.append(klin_new)
        hiddens.append(h1_new)

    if few:
        joined, buffers = groups, {}
    else:
        joined = [tuple(range(ctx))]
        keys, values = [jnp.concatenate(keys, axis=0)], [jnp.concatenate(values, axis=0)]
        buffers = {"pipeline_mode": pl.Buffered(1)}
    by_head = [
        pl.BlockSpec((ctx_rows * len(slots), width), lambda h: (0, h), **buffers) for slots in joined
    ]
    n = len(joined)
    copies = [pltpu.VMEM((seq_rows if few else 16, width), BF)] * 2
    lanes = group_width // width * half
    t_block = pl.BlockSpec((group_width, ctx_rows), lambda h: (h, 0))
    wo_block = pl.BlockSpec((group_width, model), lambda h: (h, 0))
    sums_block = pl.BlockSpec((1, 2, lanes), lambda h: (h, 0, 0))
    pair_flops = 2 * q_width * ctx_rows * seq_rows
    ot, att_t, sums, *o_parts = call(
        lambda *refs: attend_kernel(joined, ctx_rows, width, mp, *refs),
        [block_order, last_block, kpos, qpos, qlow, qt, o_weight] + keys + values,
        [
            out((q_width, ctx_rows), F32),
            out((q_width, ctx_rows), BF),
            out((kv_heads, 2, lanes), F32),
            out((share, model), F32),
        ]
        + [out((share, model), BF)] * (mp - 1),
        grid=(kv_heads,),
        in_specs={
            0: SMEM,
            1: SMEM,
            5: t_block,
            6: wo_block,
            **{7 + i: by_head[i] for i in range(n)},
            **{7 + n + i: by_head[i] for i in range(n)},
        },
        out_specs={0: t_block, 1: t_block, 2: sums_block},
        scratch=copies
        + [
            pltpu.VMEM((width, lanes), F32),
            pltpu.VMEM((1, lanes), F32),
            pltpu.VMEM((ctx_rows, model), F32),
        ],
        flops=2 * pair_flops,
        name="attend",
    )
    resid, h2_share = call(
        resid_kernel,
        [tok, o_parts[0]] + swaps(o_parts, "mp") + [gain2],
        [out((share, model), F32), out((share, model), BF)],
        name="resid",
    )

    og_late, *_ = lax.optimization_barrier((og, *[parts[-1] for parts in remote_parts]))
    grad_full = lax.all_gather(og_late, "mp", axis=0, tiled=True)
    tile = 256 if feed % 256 == 0 else feed
    col_block = pl.BlockSpec((model, tile), lambda i: (0, i))
    row_block = pl.BlockSpec((tile, model), lambda i: (i, 0))
    act_block = pl.BlockSpec((ctx_rows, tile), lambda i: (0, i))
    h2_full, og_full, act, gate_grad, up_grad, *h2_parts = call(
        lambda *refs: feed_kernel(mp, *refs),
        [peers, h2_share]
        + swaps([h2_share] * mp, "mp")
        + [grad_full, gate_weight, up_weight, down_weight],
        [out((ctx_rows, model), BF)] * 2
        + [out((ctx_rows, feed), BF)] * 3
        + [out((share, model), F32)]
        + [out((share, model), BF)] * (mp - 1),
        grid=(feed // tile,),
        in_specs={0: SMEM, mp + 2: col_block, mp + 3: col_block, mp + 4: row_block},
        out_specs={2: act_block, 3: act_block, 4: act_block},
        scratch=[pltpu.VMEM((ctx_rows, model), F32)],
        flops=10 * ctx_rows * model * feed,
        name="feed",
    )
    h2_got = swaps(h2_parts, "mp")
    dg, du, dd, *f_parts = call(
        feed_weights_kernel,
        [h2_full, og_full, act, gate_grad, up_grad, down_weight],
        [out((model, feed), BF)] * 2
        + [out((feed, model), BF), out((share, model), F32)]
        + [out((share, model), BF)] * (mp - 1),
        grid=(feed // tile,),
        in_specs={2: act_block, 3: act_block, 4: act_block, 5: row_block},
        out_specs={0: col_block, 1: col_block, 2: row_block},
        scratch=[pltpu.VMEM((ctx_rows, model), F32)],
        flops=8 * ctx_rows * model * feed,
        name="feed_weights",
    )
    h2_own, dg, du, dd = lax.optimization_barrier((h2_parts[0], dg, du, dd))
    dg, du, dd = lax.psum((dg, du, dd), ("dp", "ctx"))

    resid_grad, low_share, gain2_part = call(
        resid_back_kernel,
        [resid, og, gain2, h2_own] + h2_got,
        [out((share, model), F32), out((share, model), BF), out((1, model), F32)],
        name="resid_back",
    )
    low_parts = [low_share] + swaps([low_share] * mp, "mp")

    o_mine, o_other = call(
        o_weights_kernel,
        [here_dp[None], att_t] + low_parts,
        [out((q_width // 2, model), BF)] * 2,
        in_specs={0: SMEM},
        scratch=[pltpu.VMEM((ctx_rows, model), BF)],
        name="o_weights",
    )
    bit = ((here_ctx & 1) ^ ((here_ctx >> 1) & 1))[None]
    o_chunks = sum_over_ctx(o_mine, o_other, bit, few)
    first_low, _ = lax.optimization_barrier((low_parts[0], o_other))
    low_parts = [first_low] + low_parts[1:]
    head_rows = pl.BlockSpec((seq_rows, width), lambda h: (0, h), **buffers)
    ql, dk, dv, gq_part = call(
        lambda *refs: attend_back_kernel(joined, ctx_rows, width, mp, *refs),
        [block_order, last_block, kpos, qpos, qlow]
        + low_parts
        + [o_weight, qt, qlin, ot, sums, gq_col, cosines_t, sines_t]
        + keys
        + values,
        [
            out((q_width, ctx_rows), BF),
            out((seq_rows, k_width), F32),
            out((seq_rows, k_width), F32),
            out((width, 1), F32),
        ],
        grid=(kv_heads,),
        in_specs={
            0: SMEM,
            1: SMEM,
            5 + mp: wo_block,
            6 + mp: t_block,
            7 + mp: t_block,
            8 + mp: t_block,
            9 + mp: sums_block,
            **{13 + mp + m * n + i: by_head[i] for m in range(2) for i in range(n)},
        },
        out_specs={0: t_block, 1: head_rows, 2: head_rows},
        scratch=copies
        + [
            pltpu.VMEM((width, lanes), F32),
            pltpu.VMEM((ctx_rows, model), BF),
            pltpu.VMEM((group_width, ctx_rows), F32),
        ],
        flops=5 * pair_flops,
        name="attend_back",
    )

    f_got = swaps(f_parts, "mp")
    dk, *f_got = lax.optimization_barrier((dk, *f_got))
    output = call(
        sum_kernel, [resid, f_parts[0]] + f_got, [out((share, model), BF)], name="output"
    )[0][None]

    m = len(groups)
    starts = [sum(len(slots) for slots in groups[:i]) for i in range(m)]
    slot_at = [slot for slots in groups for slot in slots]

    def stepped(i, rows, columns):
        first, size = starts[i], len(groups[i])
        return pl.BlockSpec((rows, columns), lambda s: (jnp.clip(s - first, 0, size - 1), 0))

    def ordered(rows, columns):
        def place(s):
            slot = s
            for step, value in enumerate(slot_at):
                if step != value:
                    slot = jnp.where(s == step, value, slot)
            return slot, 0

        return pl.BlockSpec((rows, columns), place)

    kl, vl, mine, other, gain1_part, gk_part = call(
        lambda *refs: weights_kernel(groups, *refs),
        [here_dp[None], ql, dk, dv, cosines, sines, gk_row]
        + hiddens
        + klins
        + [q_weight, key_matrix, value_matrix, norm1_gain.astype(F32)[:, None]],
        [out((seq_rows, k_width), BF)] * 2
        + [out((model // 2, q_width + 2 * k_width), BF)] * 2
        + [out((model, 1), F32), out((1, width), F32)],
        grid=(ctx,),
        in_specs={
            0: SMEM,
            2: ordered(ctx_rows, k_width),
            3: ordered(ctx_rows, k_width),
            4: ordered(ctx_rows, width),
            5: ordered(ctx_rows, width),
            **{7 + i: stepped(i, ctx_rows, model) for i in range(m)},
            **{7 + m + i: stepped(i, ctx_rows, k_width) for i in range(m)},
        },
        out_specs={0: ordered(ctx_rows, k_width), 1: ordered(ctx_rows, k_width)},
        scratch=[pltpu.VMEM((model, q_width + 2 * k_width), F32)],
        name="weights",
    )

    def hidden_back(slots):
        size = len(slots)
        own = slots == (0,)
        ins = ([ql, q_weight] if own else []) + [kl, vl, key_matrix, value_matrix]
        skip = 2 if own else 0
        block = slot_blocks(slots, ctx_rows, k_width)
        parts = call(
            lambda *refs: hidden_back_kernel(own, mp, *refs),
            ins,
            [out((size, share, model), F32)] + [out((size, share, model), BF)] * (mp - 1),
            grid=(size,),
            in_specs={skip: block, skip + 1: block},
            out_specs={
                j: pl.BlockSpec((1, share, model), lambda i: (i, 0, 0)) for j in range(mp)
            },
            name="hidden_back",
        )
        return parts, swaps(parts, "mp")

    terms = []
    if few:
        for slots in ((2,), (1, 3)):
            parts, got = hidden_back(slots)
            for i, slot in enumerate(slots):
                summed = sum_parts([p[i] for p in [parts[0]] + got], BF)
                terms.append(to_ctx(summed, slot))
    else:
        parts, got = hidden_back(tuple(range(1, ctx)))
        summed = (parts[0] + sum(p.astype(F32) for p in got)).astype(BF)
        padded = jnp.concatenate([jnp.zeros_like(summed[:1]), summed], axis=0)
        padded = jnp.concatenate([padded, padded], axis=0)
        natural = lax.dynamic_slice_in_dim(padded, (ctx - here_ctx) % ctx, ctx, 0)
        terms.append(lax.psum_scatter(natural, "ctx", scatter_dimension=0, tiled=False))
    parts, got = hidden_back((0,))
    chunks = sum_over_ctx(mine, other, bit, few, (dg, du, dd, got[-1]))
    terms = [p[0] for p in [parts[0]] + got] + terms
    input_grad = call(
        input_back_kernel, [tok, resid_grad, gain1] + terms, [out((share, model), F32)], name="input_back"
    )[0][None]

    if few:
        spots = jnp.concatenate([bit, 1 - bit]) + 2 * here_dp
        spots = jnp.concatenate([spots, jnp.concatenate([bit, 1 - bit]) + 2 * (1 - here_dp)])
    else:
        spots = jnp.stack([here_dp, 1 - here_dp])
    q_w_grad, k_w_grad, v_w_grad, o_w_grad = call(
        lambda *refs: spread_kernel(q_width, k_width, len(chunks), *refs),
        [spots] + chunks + o_chunks,
        [
            out((model, q_width), F32),
            out((model, k_width), F32),
            out((model, k_width), F32),
            out((q_width, model), F32),
        ],
        in_specs={0: SMEM},
        name="spread",
    )

    gains = jnp.concatenate(
        [gain1_part.reshape(-1), gain2_part.reshape(-1), gq_part.reshape(-1), gk_part.reshape(-1)]
    )
    if few:
        for axis in ("dp", "mp", "ctx"):
            for step in (1, 2, 4):
                if step < lax.axis_size(axis):
                    gains = gains + swap(gains, axis, step)
    else:
        gains = lax.psum(gains, ("dp", "ctx", "mp"))
    return (
        output,
        input_grad,
        gains[:model],
        q_w_grad,
        k_w_grad,
        v_w_grad,
        gains[2 * model : 2 * model + width],
        gains[2 * model + width :],
        o_w_grad,
        gains[model : 2 * model],
        dg.astype(F32),
        du.astype(F32),
        dd.astype(F32),
    )


def solution(mesh):
    placed = (
        P("dp", ("ctx", "mp"), None),
        P(),
        P(None, "mp"),
        P(None, "mp"),
        P(None, "mp"),
        P(),
        P(),
        P("mp", None),
        P(),
        P(None, "mp"),
        P(None, "mp"),
        P("mp", None),
        P("dp", ("ctx", "mp"), None),
        P("dp", None),
        P(),
    )
    return jax.shard_map(
        on_device,
        mesh=mesh,
        in_specs=placed,
        out_specs=(
            P("dp", ("ctx", "mp"), None),
            P("dp", ("ctx", "mp"), None),
            P(),
            P(None, "mp"),
            P(None, "mp"),
            P(None, "mp"),
            P(),
            P(),
            P("mp", None),
            P(),
            P(None, "mp"),
            P(None, "mp"),
            P("mp", None),
        ),
        check_vma=False,
    )
```

```python
import math

import jax
import jax.numpy as jnp
from jax import lax
from jax.experimental import pallas as pl
from jax.experimental.pallas import tpu as pltpu
from jax.sharding import PartitionSpec as P

EPS = 1e-06
THETA = 1000000.0
LOG2E = 1.4426950408889634
BF = jnp.bfloat16
F32 = jnp.float32
VMEM_LIMIT = 52 * 1024 * 1024


def dot(left, right, left_dim, right_dim):
    return lax.dot_general(
        left, right, (((left_dim,), (right_dim,)), ((), ())), preferred_element_type=F32
    )


def whole_spec(array):
    rank = len(array.shape)
    return pl.BlockSpec(array.shape, lambda *_: (0,) * rank)


SMEM = pl.BlockSpec(memory_space=pltpu.SMEM)


def call(kernel, ins, outs, grid=(1,), in_specs=None, out_specs=None, scratch=(), flops=0, name=None):
    in_specs = in_specs or {}
    out_specs = out_specs or {}
    return pl.pallas_call(
        kernel,
        grid=grid,
        in_specs=[in_specs.get(i, whole_spec(a)) for i, a in enumerate(ins)],
        out_specs=[out_specs.get(i, whole_spec(a)) for i, a in enumerate(outs)],
        out_shape=list(outs),
        scratch_shapes=list(scratch),
        compiler_params=pltpu.CompilerParams(vmem_limit_bytes=VMEM_LIMIT),
        cost_estimate=pl.CostEstimate(flops=0, bytes_accessed=0, transcendentals=0),
        name=name,
    )(*ins)


def out(shape, dtype):
    return jax.ShapeDtypeStruct(shape, dtype)


def swap(value, axis, step):
    size = lax.axis_size(axis)
    return lax.ppermute(value, axis, [(i, i ^ step) for i in range(size)])


def swaps(values, axis):
    order = sorted(range(1, len(values)), key=lambda j: -bin(j).count("1"))
    got = {j: swap(values[j], axis, j) for j in order}
    return [got[j] for j in range(1, len(values))]


def from_ctx(value, step):
    size = lax.axis_size("ctx")
    return lax.ppermute(value, "ctx", [((i + step) % size, i) for i in range(size)])


def to_ctx(value, step):
    size = lax.axis_size("ctx")
    return lax.ppermute(value, "ctx", [(i, (i + step) % size) for i in range(size)])


def norm_kernel(rows_ref, gain_ref, normed_ref):
    rows = rows_ref[...].astype(F32)
    factor = lax.rsqrt(jnp.mean(rows * rows, axis=-1, keepdims=True) + EPS)
    normed_ref[...] = (rows * factor * gain_ref[...]).astype(BF)


def resid_kernel(tok_ref, own_ref, *refs):
    *parts, gain_ref, resid_ref, normed_ref = refs
    rows = tok_ref[...].astype(F32) + own_ref[...]
    for part in parts:
        rows = rows + part[...].astype(F32)
    resid_ref[...] = rows
    factor = lax.rsqrt(jnp.mean(rows * rows, axis=-1, keepdims=True) + EPS)
    normed_ref[...] = (rows * factor * gain_ref[...]).astype(BF)


def norm_back(rows, gain, gradient):
    factor = lax.rsqrt(jnp.mean(rows * rows, axis=-1, keepdims=True) + EPS)
    scaled = gradient * gain
    inner = jnp.mean(scaled * rows, axis=-1, keepdims=True)
    return factor * scaled - rows * (factor * factor * factor) * inner, gradient * rows * factor


def resid_back_kernel(resid_ref, grad_ref, gain_ref, own_ref, *refs):
    *parts, full_ref, low_ref, gain_grad_ref = refs
    gradient = own_ref[...]
    for part in parts:
        gradient = gradient + part[...].astype(F32)
    back, terms = norm_back(resid_ref[...], gain_ref[...], gradient)
    total = grad_ref[...].astype(F32) + back
    full_ref[...] = total
    low_ref[...] = total.astype(BF)
    gain_grad_ref[...] = jnp.sum(terms, axis=0, keepdims=True)


def input_back_kernel(tok_ref, resid_grad_ref, gain_ref, *refs):
    *parts, result_ref = refs
    gradient = parts[0][...].astype(F32)
    for part in parts[1:]:
        gradient = gradient + part[...].astype(F32)
    back, _ = norm_back(tok_ref[...].astype(F32), gain_ref[...], gradient)
    result_ref[...] = resid_grad_ref[...] + back


def sum_kernel(*refs):
    *parts, result_ref = refs
    total = parts[0][...].astype(F32)
    for part in parts[1:]:
        total = total + part[...].astype(F32)
    result_ref[...] = total.astype(result_ref.dtype)


def sum_parts(parts, dtype):
    return call(sum_kernel, parts, [out(parts[0].shape, dtype)], name="sum_parts")[0]


def key_rows(linear, gain, cosines, sines):
    heads = []
    for start in range(0, linear.shape[1], gain.shape[1]):
        rows = linear[:, start : start + gain.shape[1]]
        factor = lax.rsqrt(jnp.mean(rows * rows, axis=-1, keepdims=True) + EPS)
        normed = rows * factor * gain
        turned = pltpu.roll(normed, normed.shape[1] // 2, 1)
        heads.append((normed * cosines + turned * sines).astype(BF))
    return heads


def key_value_part(hidden, wk_ref, wv_ref, gk_ref, cos_ref, sin_ref, k_ref, v_ref, klin_ref):
    linear = dot(hidden, wk_ref[...], 1, 0)
    klin_ref[...] = linear
    width = gk_ref.shape[1]
    for head, rows in enumerate(key_rows(linear, gk_ref[...], cos_ref[...], sin_ref[...])):
        k_ref[:, head * width : (head + 1) * width] = rows
    v_ref[...] = dot(hidden, wv_ref[...], 1, 0).astype(BF)


def turn_rows(value):
    half = value.shape[0] // 2
    return jnp.concatenate([-value[half:], value[:half]], axis=0)


def own_kernel(count, *refs):
    parts = refs[:count]
    (wq_ref, wk_ref, wv_ref, gq_ref, gk_ref, cos_t_ref, sin_t_ref, cos_ref, sin_ref) = refs[
        count : count + 9
    ]
    qt_ref, qlin_ref, k_ref, v_ref, klin_ref, hidden_ref = refs[count + 9 :]
    share = parts[0].shape[0]
    for j, part in enumerate(parts):
        hidden_ref[j * share : (j + 1) * share, :] = part[...]
    hidden = hidden_ref[...]
    key_value_part(hidden, wk_ref, wv_ref, gk_ref, cos_ref, sin_ref, k_ref, v_ref, klin_ref)
    linear = dot(wq_ref[...], hidden, 0, 1)
    qlin_ref[...] = linear
    width = gq_ref.shape[0]
    for start in range(0, linear.shape[0], width):
        rows = linear[start : start + width]
        factor = lax.rsqrt(jnp.mean(rows * rows, axis=0, keepdims=True) + EPS)
        normed = rows * factor * gq_ref[...]
        qt_ref[start : start + width, :] = (
            normed * cos_t_ref[...] + turn_rows(normed) * sin_t_ref[...]
        ).astype(BF)


def remote_kernel(count, *refs):
    parts = refs[:count]
    wk_ref, wv_ref, gk_ref, cos_ref, sin_ref = refs[count : count + 5]
    k_ref, v_ref, klin_ref, hidden_ref = refs[count + 5 :]
    share = parts[0].shape[1]
    for j, part in enumerate(parts):
        hidden_ref[j * share : (j + 1) * share, :] = part[0]
    key_value_part(
        hidden_ref[...], wk_ref, wv_ref, gk_ref, cos_ref, sin_ref, k_ref, v_ref, klin_ref
    )


def place_slots(target_ref, refs, groups, rows):
    if len(refs) == 1:
        return refs[0]
    for ref, group in zip(refs, groups):
        for i, slot in enumerate(group):
            target_ref[pl.ds(slot * rows, rows), :] = ref[i * rows : (i + 1) * rows, :]
    return target_ref


def lanes_of(ref, half_index, half, width):
    heads = [
        ref[start : start + width, half_index * half : (half_index + 1) * half]
        for start in range(0, ref.shape[0], width)
    ]
    return jnp.concatenate(heads, axis=1)


def attend_kernel(groups, ctx_rows, width, mp, *refs):
    n = len(groups)
    order_ref, last_ref, kpos_ref, qpos_ref, qlow_ref, qt_ref, wo_ref = refs[:7]
    k_refs, v_refs = refs[7 : 7 + n], refs[7 + n : 7 + 2 * n]
    rest = refs[7 + 2 * n :]
    ot_ref, attt_ref, sums_ref = rest[:3]
    part_refs = rest[3 : 3 + mp]
    k_all, v_all, numer, sums, projected = rest[3 + mp :]
    half = ctx_rows // 2
    share = ctx_rows // mp
    per_group = qt_ref.shape[0] // width
    k_all = place_slots(k_all, k_refs, groups, ctx_rows)
    v_all = place_slots(v_all, v_refs, groups, ctx_rows)
    scale = LOG2E / math.sqrt(width)
    for t in range(2):
        queries = lanes_of(qt_ref, t, half, width)
        qpos = jnp.concatenate([qpos_ref[:, t * half : (t + 1) * half]] * per_group, axis=1)
        qlow = jnp.concatenate([qlow_ref[:, t * half : (t + 1) * half]] * per_group, axis=1)
        numer[...] = jnp.zeros_like(numer)
        sums[...] = jnp.zeros_like(sums)

        def block(i):
            start = pl.multiple_of(order_ref[i] * half, half)
            scores = dot(k_all[pl.ds(start, half), :], queries, 1, 0)
            kpos = kpos_ref[...] + i * half
            seen = (kpos <= qpos) & (kpos >= qlow)
            weights = jnp.where(seen, jnp.exp2(scores * scale), 0.0)
            added = dot(v_all[pl.ds(start, half), :], weights.astype(BF), 0, 0)
            return jnp.sum(weights, axis=0, keepdims=True), added

        def step(i, carry):
            first_sum, first = block(2 * i)
            second_sum, second = block(2 * i + 1)
            sums[...] += first_sum + second_sum
            numer[...] += first + second
            return carry

        lax.fori_loop(0, last_ref[t] // 2 + 1, step, 0)
        total = sums[...]
        sums_ref[0, t : t + 1, :] = total
        result = numer[...] / total
        for head in range(per_group):
            piece = result[:, head * half : (head + 1) * half]
            ot_ref[head * width : (head + 1) * width, t * half : (t + 1) * half] = piece
            attt_ref[head * width : (head + 1) * width, t * half : (t + 1) * half] = piece.astype(BF)
    added = dot(attt_ref[...], wo_ref[...], 0, 0)
    group = pl.program_id(0)

    @pl.when(group == 0)
    def _():
        projected[...] = added

    @pl.when(group > 0)
    def _():
        projected[...] += added

    @pl.when(group == pl.num_programs(0) - 1)
    def _():
        for j, ref in enumerate(part_refs):
            ref[...] = projected[j * share : (j + 1) * share, :].astype(ref.dtype)


def feed_kernel(count, *refs):
    peer_ref = refs[0]
    parts = refs[1 : 1 + count]
    grad_ref, wg_ref, wu_ref, wd_ref = refs[1 + count : 5 + count]
    hidden_ref, grads_ref, act_ref, gg_ref, ug_ref = refs[5 + count : 10 + count]
    part_refs = refs[10 + count : 10 + 2 * count]
    total = refs[10 + 2 * count]
    share = parts[0].shape[0]
    step = pl.program_id(0)

    @pl.when(step == 0)
    def _():
        for j, part in enumerate(parts):
            hidden_ref[j * share : (j + 1) * share, :] = part[...]
            place = pl.multiple_of(peer_ref[j] * share, share)
            grads_ref[j * share : (j + 1) * share, :] = grad_ref[pl.ds(place, share), :]

    hidden = hidden_ref[...]
    tile = wg_ref.shape[1]
    both = jnp.concatenate([wg_ref[...], wu_ref[...]], axis=1)
    product = dot(hidden, both, 1, 0)
    gate, up = product[:, :tile], product[:, tile:]
    act_grad = dot(grads_ref[...], wd_ref[...], 1, 1)
    sig = 0.5 * jnp.tanh(0.5 * gate) + 0.5
    silu = gate * sig
    act_ref[...] = (silu * up).astype(BF)
    gate_grad = (act_grad * up * sig * (1.0 + gate * (1.0 - sig))).astype(BF)
    up_grad = (act_grad * silu).astype(BF)
    gg_ref[...] = gate_grad
    ug_ref[...] = up_grad
    added = dot(jnp.concatenate([gate_grad, up_grad], axis=1), both, 1, 1)

    @pl.when(step == 0)
    def _():
        total[...] = added

    @pl.when(step > 0)
    def _():
        total[...] += added

    @pl.when(step == pl.num_programs(0) - 1)
    def _():
        for j, ref in enumerate(part_refs):
            ref[...] = total[j * share : (j + 1) * share, :].astype(ref.dtype)


def feed_weights_kernel(hidden_ref, grads_ref, act_ref, gg_ref, ug_ref, wd_ref, *refs):
    dg_ref, du_ref, dd_ref = refs[:3]
    *part_refs, total = refs[3:]
    share = part_refs[0].shape[0]
    step = pl.program_id(0)
    dg_ref[...] = dot(hidden_ref[...], gg_ref[...], 0, 0).astype(BF)
    du_ref[...] = dot(hidden_ref[...], ug_ref[...], 0, 0).astype(BF)
    dd_ref[...] = dot(act_ref[...], grads_ref[...], 0, 0).astype(BF)
    added = dot(act_ref[...], wd_ref[...], 1, 0)

    @pl.when(step == 0)
    def _():
        total[...] = added

    @pl.when(step > 0)
    def _():
        total[...] += added

    @pl.when(step == pl.num_programs(0) - 1)
    def _():
        for j, ref in enumerate(part_refs):
            ref[...] = total[j * share : (j + 1) * share, :].astype(ref.dtype)


def attend_back_kernel(groups, ctx_rows, width, mp, *refs):
    n = len(groups)
    order_ref, last_ref, kpos_ref, qpos_ref, qlow_ref = refs[:5]
    low_refs = refs[5 : 5 + mp]
    wo_ref, qt_ref, qlin_ref, ot_ref, sums_ref, gq_ref, cos_t_ref, sin_t_ref = refs[
        5 + mp : 13 + mp
    ]
    at = 13 + mp
    k_refs, v_refs = refs[at : at + n], refs[at + n : at + 2 * n]
    at += 2 * n
    ql_ref, dk, dv, gqg_ref = refs[at : at + 4]
    k_all, v_all, dq, low_all, dqt = refs[at + 4 :]
    half = ctx_rows // 2
    share = ctx_rows // mp
    per_group = qt_ref.shape[0] // width
    scale = LOG2E / math.sqrt(width)
    score_scale = 1.0 / math.sqrt(width)
    group = pl.program_id(0)
    k_all = place_slots(k_all, k_refs, groups, ctx_rows)
    v_all = place_slots(v_all, v_refs, groups, ctx_rows)
    dk[...] = jnp.zeros_like(dk)
    dv[...] = jnp.zeros_like(dv)

    @pl.when(group == 0)
    def _():
        for j, ref in enumerate(low_refs):
            low_all[j * share : (j + 1) * share, :] = ref[...]
        gqg_ref[...] = jnp.zeros_like(gqg_ref)

    att_grad = dot(wo_ref[...], low_all[...], 1, 1).astype(BF).astype(F32)
    for t in range(2):
        queries = lanes_of(qt_ref, t, half, width)
        pre = lanes_of(ot_ref, t, half, width)
        grads = jnp.concatenate(
            [
                att_grad[h * width : (h + 1) * width, t * half : (t + 1) * half]
                for h in range(per_group)
            ],
            axis=1,
        )
        inverse = 1.0 / sums_ref[0, t : t + 1, :]
        scaled = (grads * inverse).astype(BF)
        shift = jnp.sum(grads * pre, axis=0, keepdims=True) * inverse
        qpos = jnp.concatenate([qpos_ref[:, t * half : (t + 1) * half]] * per_group, axis=1)
        qlow = jnp.concatenate([qlow_ref[:, t * half : (t + 1) * half]] * per_group, axis=1)
        dq[...] = jnp.zeros_like(dq)

        def block(i):
            start = pl.multiple_of(order_ref[i] * half, half)
            keys = k_all[pl.ds(start, half), :]
            scores = dot(keys, queries, 1, 0)
            prob_grad = dot(v_all[pl.ds(start, half), :], scaled, 1, 0)
            kpos = kpos_ref[...] + i * half
            seen = (kpos <= qpos) & (kpos >= qlow)
            weights = jnp.where(seen, jnp.exp2(scores * scale), 0.0)
            score_grad = (weights * (prob_grad - shift)).astype(BF)
            dv[pl.ds(start, half), :] += dot(weights.astype(BF), scaled, 1, 1)
            dk[pl.ds(start, half), :] += dot(score_grad, queries, 1, 1)
            return dot(keys, score_grad, 0, 0)

        def step(i, carry):
            first = block(2 * i)
            dq[...] += first + block(2 * i + 1)
            return carry

        lax.fori_loop(0, last_ref[t] // 2 + 1, step, 0)
        for head in range(per_group):
            dqt[head * width : (head + 1) * width, t * half : (t + 1) * half] = dq[
                :, head * half : (head + 1) * half
            ]
    for head in range(per_group):
        rows = qlin_ref[head * width : (head + 1) * width, :]
        rotated = dqt[head * width : (head + 1) * width, :] * score_scale
        gradient = rotated * cos_t_ref[...] - turn_rows(rotated) * sin_t_ref[...]
        factor = lax.rsqrt(jnp.mean(rows * rows, axis=0, keepdims=True) + EPS)
        gained = gradient * gq_ref[...]
        inner = jnp.mean(gained * rows, axis=0, keepdims=True)
        ql_ref[head * width : (head + 1) * width, :] = (
            factor * gained - rows * (factor * factor * factor) * inner
        ).astype(BF)
        gqg_ref[...] += jnp.sum(gradient * rows * factor, axis=1, keepdims=True)


def hidden_back_kernel(own, mp, *refs):
    if own:
        ql_ref, wq_ref, *refs = refs
    kl_ref, vl_ref, wk_ref, wv_ref = refs[:4]
    part_refs = refs[4:]
    share = part_refs[0].shape[1]
    total = dot(kl_ref[...], wk_ref[...], 1, 1) + dot(vl_ref[...], wv_ref[...], 1, 1)
    if own:
        total = total + dot(ql_ref[...], wq_ref[...], 0, 1)
    for j, ref in enumerate(part_refs):
        ref[0] = total[j * share : (j + 1) * share, :].astype(ref.dtype)


def o_weights_kernel(core_ref, attt_ref, *refs):
    *low_refs, mine_ref, other_ref, low_all = refs
    share = low_refs[0].shape[0]
    for j, ref in enumerate(low_refs):
        low_all[j * share : (j + 1) * share, :] = ref[...]
    rows = mine_ref.shape[0]
    core = core_ref[0]
    for ref, at in ((mine_ref, core), (other_ref, 1 - core)):
        here = pl.ds(pl.multiple_of(at * rows, rows), rows)
        ref[...] = dot(attt_ref[here, :], low_all[...], 1, 0).astype(BF)


def weights_kernel(groups, *refs):
    n = len(groups)
    core_ref, ql_ref, dk_ref, dv_ref, cos_ref, sin_ref, gk_ref = refs[:7]
    hidden_refs, klin_refs = refs[7 : 7 + n], refs[7 + n : 7 + 2 * n]
    (
        wq_ref, wk_ref, wv_ref, gain_ref, kl_ref, vl_ref,
        mine_ref, other_ref, gain_grad_ref, gkg_ref, accum,
    ) = refs[7 + 2 * n :]
    step = pl.program_id(0)
    model = gain_ref.shape[0]
    q_width, k_width = ql_ref.shape[0], dk_ref.shape[1]
    width = gk_ref.shape[1]
    score_scale = 1.0 / math.sqrt(width)

    @pl.when(step == 0)
    def _():
        accum[:, :q_width] = dot(hidden_refs[0][...], ql_ref[...], 0, 1)
        accum[:, q_width:] = jnp.zeros_like(accum[:, q_width:])
        gkg_ref[...] = jnp.zeros_like(gkg_ref)

    first = 0
    for hidden_ref, klin_ref, slots in zip(hidden_refs, klin_refs, groups):

        @pl.when((step >= first) & (step < first + len(slots)))
        def _():
            for start in range(0, k_width, width):
                head = slice(start, start + width)
                rotated = dk_ref[:, head] * score_scale
                gradient = rotated * cos_ref[...] - pltpu.roll(rotated, width // 2, 1) * sin_ref[...]
                back, terms = norm_back(klin_ref[:, head], gk_ref[...], gradient)
                kl_ref[:, head] = back.astype(BF)
                gkg_ref[...] += jnp.sum(terms, axis=0, keepdims=True)
            vl_ref[...] = dv_ref[...].astype(BF)
            hidden = hidden_ref[...]
            accum[:, q_width : q_width + k_width] += dot(hidden, kl_ref[...], 0, 0)
            accum[:, q_width + k_width :] += dot(hidden, vl_ref[...], 0, 0)

        first += len(slots)

    @pl.when(step == pl.num_programs(0) - 1)
    def _():
        terms = jnp.sum(accum[:, :q_width] * wq_ref[...].astype(F32), axis=1, keepdims=True)
        terms += jnp.sum(
            accum[:, q_width : q_width + k_width] * wk_ref[...].astype(F32), axis=1, keepdims=True
        )
        terms += jnp.sum(
            accum[:, q_width + k_width :] * wv_ref[...].astype(F32), axis=1, keepdims=True
        )
        gain_grad_ref[...] = terms / gain_ref[...]
        rows = mine_ref.shape[0]
        core = core_ref[0]
        mine_ref[...] = accum[pl.ds(pl.multiple_of(core * rows, rows), rows), :].astype(BF)
        other_ref[...] = accum[pl.ds(pl.multiple_of((1 - core) * rows, rows), rows), :].astype(BF)


def split_kernel(place_ref, mine_ref, got_ref, keep_ref, send_ref):
    rows = keep_ref.shape[0]
    for ref, at in ((keep_ref, place_ref[0]), (send_ref, 1 - place_ref[0])):
        here = pl.ds(pl.multiple_of(at * rows, rows), rows)
        ref[...] = (mine_ref[here, :].astype(F32) + got_ref[here, :].astype(F32)).astype(ref.dtype)


def spread_kernel(q_width, k_width, count, *refs):
    place_ref = refs[0]
    chunks, o_chunks = refs[1 : 1 + count], refs[1 + count : 1 + 2 * count]
    dq_ref, dk_ref, dv_ref, do_ref = refs[1 + 2 * count :]
    for i, ref in enumerate(chunks):
        rows = ref.shape[0]
        here = pl.ds(pl.multiple_of(place_ref[i] * rows, rows), rows)
        dq_ref[here, :] = ref[:, :q_width].astype(F32)
        dk_ref[here, :] = ref[:, q_width : q_width + k_width].astype(F32)
        dv_ref[here, :] = ref[:, q_width + k_width :].astype(F32)
    for i, ref in enumerate(o_chunks):
        rows = ref.shape[0]
        here = pl.ds(pl.multiple_of(place_ref[i] * rows, rows), rows)
        do_ref[here, :] = ref[...].astype(F32)


def sum_over_ctx(mine, other, part, few, after=()):
    got = swap(other, "dp", 1)
    if not few:
        chunk = lax.psum(sum_parts([mine, got], BF), "ctx")
        return [chunk, swap(chunk, "dp", 1)]
    rows = mine.shape[0] // 2
    keep, send = call(
        split_kernel,
        [part, mine, got],
        [out((rows, mine.shape[1]), F32), out((rows, mine.shape[1]), BF)],
        in_specs={0: SMEM},
        name="split",
    )
    pair = sum_parts([keep, swap(send, "ctx", 1)], BF)
    if after:
        pair, *_ = lax.optimization_barrier((pair, *after))
    total = sum_parts([pair, swap(pair, "ctx", 3)], BF)
    far = swap(total, "ctx", 1)
    near = total
    if after:
        near, *_ = lax.optimization_barrier((total, *[a.astype(F32) for a in after[:3]]))
    return [total, far, swap(near, "dp", 1), swap(far, "dp", 1)]


def slot_blocks(group, rows, width):
    first = group[0]
    gap = group[1] - group[0] if len(group) > 1 else 1
    return pl.BlockSpec((rows, width), lambda i: (first + gap * i, 0))


def on_device(
    tokens,
    norm1_gain,
    q_weight,
    key_matrix,
    value_matrix,
    q_gain,
    k_gain,
    o_weight,
    norm2_gain,
    gate_weight,
    up_weight,
    down_weight,
    out_grad,
    lengths,
    pairing,
):
    width = q_gain.shape[0]
    model = tokens.shape[2]
    share = tokens.shape[1]
    mp = lax.axis_size("mp")
    ctx = lax.axis_size("ctx")
    q_width = q_weight.shape[1]
    k_width = key_matrix.shape[1]
    kv_heads = k_width // width
    group_width = q_width // kv_heads
    feed = gate_weight.shape[1]
    ctx_rows = share * mp
    half = ctx_rows // 2
    seq_rows = ctx_rows * ctx
    few = ctx == 4
    here_ctx = lax.axis_index("ctx")
    here_mp = lax.axis_index("mp")
    here_dp = lax.axis_index("dp")
    gain1 = norm1_gain.astype(F32)[None, :]
    gain2 = norm2_gain.astype(F32)[None, :]
    gq_col = q_gain.astype(F32)[:, None]
    gk_row = k_gain.astype(F32)[None, :]
    tok = tokens[0]
    og = out_grad[0]

    h1_share = call(norm_kernel, [tok, gain1], [out((share, model), BF)], name="norm1")[0]
    own_parts = [h1_share] + swaps([h1_share] * mp, "mp")
    if few:
        near = {k: from_ctx(h1_share, k) for k in (1, 3)}
        own_parts[0], near[1], near[3] = lax.optimization_barrier((own_parts[0], near[1], near[3]))

    slot_ctx = (here_ctx + jnp.arange(ctx, dtype=jnp.int32)) % ctx
    slot_pair = jnp.sum(
        jnp.where(slot_ctx[:, None] == jnp.arange(ctx, dtype=jnp.int32)[None, :], pairing[None, :], 0),
        axis=1,
    )
    peers = here_mp ^ jnp.arange(mp, dtype=jnp.int32)
    rows_in = (peers[:, None] * share + jnp.arange(share, dtype=jnp.int32)[None, :]).reshape(-1)
    blocks = jnp.where(
        rows_in[None, :] < half, slot_pair[:, None], 2 * ctx - 1 - slot_pair[:, None]
    )
    positions = (blocks * half + (rows_in % half)[None, :]).reshape(-1)
    block_ids = blocks[:, ::half].reshape(-1)
    block_order = jnp.sum(
        jnp.where(
            block_ids[None, :] == jnp.arange(2 * ctx, dtype=jnp.int32)[:, None],
            jnp.arange(2 * ctx, dtype=jnp.int32)[None, :],
            0,
        ),
        axis=1,
    )
    last_block = block_ids[:2]
    own_pos = positions[:ctx_rows]
    doc_ends = jnp.cumsum(lengths[0])
    own_low = jnp.max(
        jnp.where(doc_ends[None, :] <= own_pos[:, None], doc_ends[None, :], 0), axis=1
    )
    qpos, qlow, kpos = own_pos[None, :], own_low[None, :], (rows_in % half)[:half, None]
    frequency = THETA ** (-(jnp.arange(width // 2, dtype=F32) * 2.0) / width)
    angles = positions.astype(F32)[:, None] * frequency[None, :]
    cos_half, sin_half = jnp.cos(angles), jnp.sin(angles)
    cosines = jnp.concatenate([cos_half, cos_half], axis=1)
    sines = jnp.concatenate([-sin_half, sin_half], axis=1)
    angles_t = frequency[:, None] * own_pos.astype(F32)[None, :]
    cos_t, sin_t = jnp.cos(angles_t), jnp.sin(angles_t)
    cosines_t = jnp.concatenate([cos_t, cos_t], axis=0)
    sines_t = jnp.concatenate([sin_t, sin_t], axis=0)

    qt, qlin, k_own, v_own, klin_own, h1_own = call(
        lambda *refs: own_kernel(mp, *refs),
        own_parts
        + [q_weight, key_matrix, value_matrix, gq_col, gk_row, cosines_t, sines_t, cosines, sines],
        [
            out((q_width, ctx_rows), BF),
            out((q_width, ctx_rows), F32),
            out((ctx_rows, k_width), BF),
            out((ctx_rows, k_width), BF),
            out((ctx_rows, k_width), F32),
            out((ctx_rows, model), BF),
        ],
        in_specs={
            mp + 7: pl.BlockSpec((ctx_rows, width), lambda i: (0, 0)),
            mp + 8: pl.BlockSpec((ctx_rows, width), lambda i: (0, 0)),
        },
        flops=2 * ctx_rows * model * (q_width + 2 * k_width),
        name="own_rows",
    )
    if few:
        late_share, _ = lax.optimization_barrier((h1_share, k_own))
        far = from_ctx(late_share, 2)
        remote = [((1, 3), jnp.stack([near[1], near[3]])), ((2,), far[None])]
    else:
        every = lax.all_gather(h1_share, "ctx", axis=0)
        every = jnp.concatenate([every, every], axis=0)
        every = lax.dynamic_slice_in_dim(every, here_ctx + 1, ctx - 1, 0)
        remote = [(tuple(range(1, ctx)), every)]
    remote_parts = [[value] + swaps([value] * mp, "mp") for _, value in remote]
    groups = [(0,)] + [slots for slots, _ in remote]
    keys, values, klins, hiddens = [k_own], [v_own], [klin_own], [h1_own]
    for (slots, _), parts in zip(remote, remote_parts):
        size = len(slots)
        k_new, v_new, klin_new, h1_new = call(
            lambda *refs: remote_kernel(mp, *refs),
            parts + [key_matrix, value_matrix, gk_row, cosines, sines],
            [
                out((size * ctx_rows, k_width), BF),
                out((size * ctx_rows, k_width), BF),
                out((size * ctx_rows, k_width), F32),
                out((size * ctx_rows, model), BF),
            ],
            grid=(size,),
            in_specs={
                **{j: pl.BlockSpec((1, share, model), lambda i: (i, 0, 0)) for j in range(mp)},
                mp + 3: slot_blocks(slots, ctx_rows, width),
                mp + 4: slot_blocks(slots, ctx_rows, width),
            },
            out_specs={
                0: pl.BlockSpec((ctx_rows, k_width), lambda i: (i, 0)),
                1: pl.BlockSpec((ctx_rows, k_width), lambda i: (i, 0)),
                2: pl.BlockSpec((ctx_rows, k_width), lambda i: (i, 0)),
                3: pl.BlockSpec((ctx_rows, model), lambda i: (i, 0)),
            },
            flops=4 * size * ctx_rows * model * k_width,
            name="remote_rows",
        )
        keys.append(k_new)
        values.append(v_new)
        klins.append(klin_new)
        hiddens.append(h1_new)

    if few:
        joined, buffers = groups, {}
    else:
        joined = [tuple(range(ctx))]
        keys, values = [jnp.concatenate(keys, axis=0)], [jnp.concatenate(values, axis=0)]
        buffers = {"pipeline_mode": pl.Buffered(1)}
    by_head = [
        pl.BlockSpec((ctx_rows * len(slots), width), lambda h: (0, h), **buffers) for slots in joined
    ]
    n = len(joined)
    copies = [pltpu.VMEM((seq_rows if few else 16, width), BF)] * 2
    lanes = group_width // width * half
    t_block = pl.BlockSpec((group_width, ctx_rows), lambda h: (h, 0))
    wo_block = pl.BlockSpec((group_width, model), lambda h: (h, 0))
    sums_block = pl.BlockSpec((1, 2, lanes), lambda h: (h, 0, 0))
    pair_flops = 2 * q_width * ctx_rows * seq_rows
    ot, att_t, sums, *o_parts = call(
        lambda *refs: attend_kernel(joined, ctx_rows, width, mp, *refs),
        [block_order, last_block, kpos, qpos, qlow, qt, o_weight] + keys + values,
        [
            out((q_width, ctx_rows), F32),
            out((q_width, ctx_rows), BF),
            out((kv_heads, 2, lanes), F32),
            out((share, model), F32),
        ]
        + [out((share, model), BF)] * (mp - 1),
        grid=(kv_heads,),
        in_specs={
            0: SMEM,
            1: SMEM,
            5: t_block,
            6: wo_block,
            **{7 + i: by_head[i] for i in range(n)},
            **{7 + n + i: by_head[i] for i in range(n)},
        },
        out_specs={0: t_block, 1: t_block, 2: sums_block},
        scratch=copies
        + [
            pltpu.VMEM((width, lanes), F32),
            pltpu.VMEM((1, lanes), F32),
            pltpu.VMEM((ctx_rows, model), F32),
        ],
        flops=2 * pair_flops,
        name="attend",
    )
    resid, h2_share = call(
        resid_kernel,
        [tok, o_parts[0]] + swaps(o_parts, "mp") + [gain2],
        [out((share, model), F32), out((share, model), BF)],
        name="resid",
    )

    og_late, *_ = lax.optimization_barrier((og, *[parts[-1] for parts in remote_parts]))
    grad_full = lax.all_gather(og_late, "mp", axis=0, tiled=True)
    tile = 256 if feed % 256 == 0 else feed
    col_block = pl.BlockSpec((model, tile), lambda i: (0, i))
    row_block = pl.BlockSpec((tile, model), lambda i: (i, 0))
    act_block = pl.BlockSpec((ctx_rows, tile), lambda i: (0, i))
    h2_full, og_full, act, gate_grad, up_grad, *h2_parts = call(
        lambda *refs: feed_kernel(mp, *refs),
        [peers, h2_share]
        + swaps([h2_share] * mp, "mp")
        + [grad_full, gate_weight, up_weight, down_weight],
        [out((ctx_rows, model), BF)] * 2
        + [out((ctx_rows, feed), BF)] * 3
        + [out((share, model), F32)]
        + [out((share, model), BF)] * (mp - 1),
        grid=(feed // tile,),
        in_specs={0: SMEM, mp + 2: col_block, mp + 3: col_block, mp + 4: row_block},
        out_specs={2: act_block, 3: act_block, 4: act_block},
        scratch=[pltpu.VMEM((ctx_rows, model), F32)],
        flops=10 * ctx_rows * model * feed,
        name="feed",
    )
    h2_got = swaps(h2_parts, "mp")
    dg, du, dd, *f_parts = call(
        feed_weights_kernel,
        [h2_full, og_full, act, gate_grad, up_grad, down_weight],
        [out((model, feed), BF)] * 2
        + [out((feed, model), BF), out((share, model), F32)]
        + [out((share, model), BF)] * (mp - 1),
        grid=(feed // tile,),
        in_specs={2: act_block, 3: act_block, 4: act_block, 5: row_block},
        out_specs={0: col_block, 1: col_block, 2: row_block},
        scratch=[pltpu.VMEM((ctx_rows, model), F32)],
        flops=8 * ctx_rows * model * feed,
        name="feed_weights",
    )
    h2_own, dg, du, dd = lax.optimization_barrier((h2_parts[0], dg, du, dd))
    dg, du, dd = lax.psum((dg, du, dd), ("dp", "ctx"))

    resid_grad, low_share, gain2_part = call(
        resid_back_kernel,
        [resid, og, gain2, h2_own] + h2_got,
        [out((share, model), F32), out((share, model), BF), out((1, model), F32)],
        name="resid_back",
    )
    low_parts = [low_share] + swaps([low_share] * mp, "mp")

    o_mine, o_other = call(
        o_weights_kernel,
        [here_dp[None], att_t] + low_parts,
        [out((q_width // 2, model), BF)] * 2,
        in_specs={0: SMEM},
        scratch=[pltpu.VMEM((ctx_rows, model), BF)],
        name="o_weights",
    )
    bit = ((here_ctx & 1) ^ ((here_ctx >> 1) & 1))[None]
    o_chunks = sum_over_ctx(o_mine, o_other, bit, few)
    first_low, _ = lax.optimization_barrier((low_parts[0], o_other))
    low_parts = [first_low] + low_parts[1:]
    head_rows = pl.BlockSpec((seq_rows, width), lambda h: (0, h), **buffers)
    ql, dk, dv, gq_part = call(
        lambda *refs: attend_back_kernel(joined, ctx_rows, width, mp, *refs),
        [block_order, last_block, kpos, qpos, qlow]
        + low_parts
        + [o_weight, qt, qlin, ot, sums, gq_col, cosines_t, sines_t]
        + keys
        + values,
        [
            out((q_width, ctx_rows), BF),
            out((seq_rows, k_width), F32),
            out((seq_rows, k_width), F32),
            out((width, 1), F32),
        ],
        grid=(kv_heads,),
        in_specs={
            0: SMEM,
            1: SMEM,
            5 + mp: wo_block,
            6 + mp: t_block,
            7 + mp: t_block,
            8 + mp: t_block,
            9 + mp: sums_block,
            **{13 + mp + m * n + i: by_head[i] for m in range(2) for i in range(n)},
        },
        out_specs={0: t_block, 1: head_rows, 2: head_rows},
        scratch=copies
        + [
            pltpu.VMEM((width, lanes), F32),
            pltpu.VMEM((ctx_rows, model), BF),
            pltpu.VMEM((group_width, ctx_rows), F32),
        ],
        flops=5 * pair_flops,
        name="attend_back",
    )

    f_got = swaps(f_parts, "mp")
    dk, *f_got = lax.optimization_barrier((dk, *f_got))
    output = call(
        sum_kernel, [resid, f_parts[0]] + f_got, [out((share, model), BF)], name="output"
    )[0][None]

    m = len(groups)
    starts = [sum(len(slots) for slots in groups[:i]) for i in range(m)]
    slot_at = [slot for slots in groups for slot in slots]

    def stepped(i, rows, columns):
        first, size = starts[i], len(groups[i])
        return pl.BlockSpec((rows, columns), lambda s: (jnp.clip(s - first, 0, size - 1), 0))

    def ordered(rows, columns):
        def place(s):
            slot = s
            for step, value in enumerate(slot_at):
                if step != value:
                    slot = jnp.where(s == step, value, slot)
            return slot, 0

        return pl.BlockSpec((rows, columns), place)

    kl, vl, mine, other, gain1_part, gk_part = call(
        lambda *refs: weights_kernel(groups, *refs),
        [here_dp[None], ql, dk, dv, cosines, sines, gk_row]
        + hiddens
        + klins
        + [q_weight, key_matrix, value_matrix, norm1_gain.astype(F32)[:, None]],
        [out((seq_rows, k_width), BF)] * 2
        + [out((model // 2, q_width + 2 * k_width), BF)] * 2
        + [out((model, 1), F32), out((1, width), F32)],
        grid=(ctx,),
        in_specs={
            0: SMEM,
            2: ordered(ctx_rows, k_width),
            3: ordered(ctx_rows, k_width),
            4: ordered(ctx_rows, width),
            5: ordered(ctx_rows, width),
            **{7 + i: stepped(i, ctx_rows, model) for i in range(m)},
            **{7 + m + i: stepped(i, ctx_rows, k_width) for i in range(m)},
        },
        out_specs={0: ordered(ctx_rows, k_width), 1: ordered(ctx_rows, k_width)},
        scratch=[pltpu.VMEM((model, q_width + 2 * k_width), F32)],
        name="weights",
    )

    def hidden_back(slots):
        size = len(slots)
        own = slots == (0,)
        ins = ([ql, q_weight] if own else []) + [kl, vl, key_matrix, value_matrix]
        skip = 2 if own else 0
        block = slot_blocks(slots, ctx_rows, k_width)
        parts = call(
            lambda *refs: hidden_back_kernel(own, mp, *refs),
            ins,
            [out((size, share, model), F32)] + [out((size, share, model), BF)] * (mp - 1),
            grid=(size,),
            in_specs={skip: block, skip + 1: block},
            out_specs={
                j: pl.BlockSpec((1, share, model), lambda i: (i, 0, 0)) for j in range(mp)
            },
            name="hidden_back",
        )
        return parts, swaps(parts, "mp")

    terms = []
    if few:
        for slots in ((2,), (1, 3)):
            parts, got = hidden_back(slots)
            for i, slot in enumerate(slots):
                summed = sum_parts([p[i] for p in [parts[0]] + got], BF)
                terms.append(to_ctx(summed, slot))
    else:
        parts, got = hidden_back(tuple(range(1, ctx)))
        summed = (parts[0] + sum(p.astype(F32) for p in got)).astype(BF)
        padded = jnp.concatenate([jnp.zeros_like(summed[:1]), summed], axis=0)
        padded = jnp.concatenate([padded, padded], axis=0)
        natural = lax.dynamic_slice_in_dim(padded, (ctx - here_ctx) % ctx, ctx, 0)
        terms.append(lax.psum_scatter(natural, "ctx", scatter_dimension=0, tiled=False))
    parts, got = hidden_back((0,))
    chunks = sum_over_ctx(mine, other, bit, few, (dg, du, dd, got[-1]))
    terms = [p[0] for p in [parts[0]] + got] + terms
    input_grad = call(
        input_back_kernel, [tok, resid_grad, gain1] + terms, [out((share, model), F32)], name="input_back"
    )[0][None]

    if few:
        spots = jnp.concatenate([bit, 1 - bit]) + 2 * here_dp
        spots = jnp.concatenate([spots, jnp.concatenate([bit, 1 - bit]) + 2 * (1 - here_dp)])
    else:
        spots = jnp.stack([here_dp, 1 - here_dp])
    q_w_grad, k_w_grad, v_w_grad, o_w_grad = call(
        lambda *refs: spread_kernel(q_width, k_width, len(chunks), *refs),
        [spots] + chunks + o_chunks,
        [
            out((model, q_width), F32),
            out((model, k_width), F32),
            out((model, k_width), F32),
            out((q_width, model), F32),
        ],
        in_specs={0: SMEM},
        name="spread",
    )

    gains = jnp.concatenate(
        [gain1_part.reshape(-1), gain2_part.reshape(-1), gq_part.reshape(-1), gk_part.reshape(-1)]
    )
    if few:
        for axis in ("dp", "mp", "ctx"):
            for step in (1, 2, 4):
                if step < lax.axis_size(axis):
                    gains = gains + swap(gains, axis, step)
    else:
        gains = lax.psum(gains, ("dp", "ctx", "mp"))
    return (
        output,
        input_grad,
        gains[:model],
        q_w_grad,
        k_w_grad,
        v_w_grad,
        gains[2 * model : 2 * model + width],
        gains[2 * model + width :],
        o_w_grad,
        gains[model : 2 * model],
        dg.astype(F32),
        du.astype(F32),
        dd.astype(F32),
    )


def solution(mesh):
    placed = (
        P("dp", ("ctx", "mp"), None),
        P(),
        P(None, "mp"),
        P(None, "mp"),
        P(None, "mp"),
        P(),
        P(),
        P("mp", None),
        P(),
        P(None, "mp"),
        P(None, "mp"),
        P("mp", None),
        P("dp", ("ctx", "mp"), None),
        P("dp", None),
        P(),
    )
    return jax.shard_map(
        on_device,
        mesh=mesh,
        in_specs=placed,
        out_specs=(
            P("dp", ("ctx", "mp"), None),
            P("dp", ("ctx", "mp"), None),
            P(),
            P(None, "mp"),
            P(None, "mp"),
            P(None, "mp"),
            P(),
            P(),
            P("mp", None),
            P(),
            P(None, "mp"),
            P(None, "mp"),
            P("mp", None),
        ),
        check_vma=False,
    )
```
